32 devices in a mesh: groups: 2 (over y), dp: 1, expert: 16 (over z, x, core).
Axes of the slice: x: 2, y: 2, z: 4, core: 2. Of those that a mesh axis runs over, the one named last changes fastest.
Arguments:
- student_input: bfloat16 [4096, 1024], P(('groups', 'dp', 'expert')), parts along dimension 0, may hold values from -6 to 6
- judge_output: bfloat16 [4096, 1024], P(('groups', 'dp', 'expert')), parts along dimension 0, may hold values from -4 to 4
- expert_ids: int32 [4096, 8], P(('groups', 'dp', 'expert')), parts along dimension 0, may hold values from 0 to 15, all different within a row; in each aligned block of 128 rows (0 to 127, 128 to 255, ...) at most 80 rows name the same one
- route_weights: float32 [4096, 8], P(('groups', 'dp', 'expert')), parts along dimension 0, may hold values from 0.02 to 0.3
- w_gate: bfloat16 [16, 384, 1024], P('expert', 'dp'), may hold values from -0.1875 to 0.1875
- w_up: bfloat16 [16, 384, 1024], P('expert', 'dp'), may hold values from -0.1875 to 0.1875
- w_down: bfloat16 [16, 384, 1024], P('expert', 'dp'), may hold values from -0.3125 to 0.3125
Outputs:
- student_output: bfloat16 [4096, 1024], P(('groups', 'dp', 'expert')), parts along dimension 0
- route_grads: float32 [4096, 8], P(('groups', 'dp', 'expert')), parts along dimension 0
- grad_gate: bfloat16 [32, 384, 1024], P(('groups', 'expert'), 'dp'), parts along dimension 0
- grad_up: bfloat16 [32, 384, 1024], P(('groups', 'expert'), 'dp'), parts along dimension 0
- grad_down: bfloat16 [32, 384, 1024], P(('groups', 'expert'), 'dp'), parts along dimension 0
The draws below stay inside these ranges and needn't reach their ends.
There are 2 independent parts, one for each index of `groups`. The reference program is written for one: setup_inputs(seed, part) draws one part's arguments, and reference() takes and returns one part's arrays. A program takes and returns all parts, laid end to end along the dimension named above; an argument that names none is the same for every part. Nothing has to cross between parts.
Inputs may be any that keep to these rules, and one draw needn't show every extreme that they name: `expert_ids`: each token names 8 different experts; among the 128 tokens of one device (aligned blocks of rows) no expert is named more than 80 times.
All inputs are finite; a program needn't handle non-finite values.
Results may differ from the reference program's by a relative error of at most 0.0075.
Values may be sent and summed in bfloat16 or wider, within the bound.
A program may use at most 64 MiB of HBM per device.

```python
import math
import jax
import jax.numpy as jnp
import numpy as np
from jax import lax

D = 1024
FF = 384
TOPK = 8
TOK_DEV = 128
EXPERTS = 16
MOST = 80
TOKENS = 2048
N_DP = 1
N_EXPERT = 16


def steps_of(stream_key, dims, split, smallest, high):
    gain = 1.0
    for axis_at, blocks in split:
        steps = jax.random.uniform(jax.random.fold_in(jax.random.fold_in(stream_key, 6), axis_at), (blocks,), jnp.float32, smallest / len(split), high / len(split))
        gain = gain * jnp.repeat(jnp.exp(steps), dims[axis_at] // blocks).reshape((-1,) + (1,) * (len(dims) - 1 - axis_at))
    return gain


def deal_out(stream_key, own, number, rows, amount, top, most, skew):
    ranking = jax.random.permutation(stream_key, amount)
    packed, usual = load_shares(amount, rows * top, most, skew, True), load_shares(amount, rows * top, most, skew, False)
    places = jnp.arange(amount)

    def named(sizes, turn):
        used = int((sizes > 0).sum())
        fixed = max(1, used // 4)
        passed = fixed + (places - fixed + turn * (used - fixed)) % max(1, amount - fixed)
        return jnp.zeros((amount,), jnp.int32).at[ranking[jnp.where(places < fixed, places, passed)]].set(jnp.asarray(sizes, jnp.int32))

    sizes = jnp.where(number % 4 == 0, named(packed, number // 4), named(usual, number - number // 4 - 1))
    mixed = jax.random.permutation(jax.random.fold_in(own, 3), amount)
    giver, taker = mixed[0:amount // 2 * 2:2], mixed[1:amount // 2 * 2:2]
    slack = jnp.minimum(sizes[giver] - 1, most - sizes[taker]) // 2
    slack = jnp.where((giver == ranking[0]) | (taker == ranking[0]) | (sizes[taker] == 0), 0, jnp.maximum(slack, 0))
    passed = jax.random.randint(jax.random.fold_in(own, 4), (amount // 2,), 0, 1 << 20) % (slack + 1)
    sizes = sizes.at[giver].add(-passed).at[taker].add(passed)
    items = jnp.searchsorted(jnp.cumsum(sizes), jnp.arange(rows * top), side="right").astype(jnp.int32)
    grid = items.reshape(top, rows).T
    grid = grid[jax.random.permutation(jax.random.fold_in(own, 1), rows)]
    turn = jax.random.randint(jax.random.fold_in(own, 2), (rows, 1), 0, top)
    return jnp.take_along_axis(grid, (jnp.arange(top)[None, :] + turn) % top, axis=1)


def load_shares(count, total, most, skew, full):
    portions = [(1 << 20) // math.isqrt(standing ** skew) + 1 for standing in range(1, count + 1)]
    largest = most if full else min(most, max(-(-total // count), total * portions[0] // sum(portions)))
    least = 1 if total - largest >= count - 1 else 0
    counts, surplus = [largest] + [least] * (count - 1), total - largest - least * (count - 1)
    while surplus > 0:
        movable = [i for i in range(1, count) if counts[i] < largest] or [i for i in range(1, count) if counts[i] < most]
        pool, remaining = sum([portions[i] for i in movable]), surplus
        for i in movable:
            addition = min(most - counts[i], max(1, remaining * portions[i] // pool), surplus)
            counts[i] = counts[i] + addition
            surplus = surplus - addition
    return np.array(counts)


def normal_values(own_key, shape, scale, limit, cuts=(), held_as=jnp.bfloat16):
    loudness = steps_of(own_key, shape, cuts, -0.22, 0.18) if cuts else 1.0
    result = jax.random.normal(own_key, shape, jnp.float32) * scale * loudness
    return jnp.minimum(jnp.maximum(result, -limit), limit).astype(held_as)


def setup_inputs(seed: int = 0, part: int = 0) -> dict:
    key_list = jax.random.split(jax.random.key(seed), 8)
    own_keys = jax.random.split(jax.random.fold_in(key_list[7], part), 8)
    student_input = normal_values(own_keys[0], (TOKENS, D), 1.0, 6.0, ((0, 16),))
    judge_output = normal_values(own_keys[1], (TOKENS, D), 0.5, 4.0, ((0, 16),))
    expert_ids_keys = jax.random.split(jax.random.fold_in(own_keys[2], 1), TOKENS // TOK_DEV)
    expert_ids_turns = jax.random.permutation(jax.random.fold_in(own_keys[2], 3), TOKENS // TOK_DEV)
    expert_ids = jax.vmap(lambda own, number: deal_out(jax.random.fold_in(own_keys[2], 2), own, number, TOK_DEV, EXPERTS, TOPK, MOST, 2))(expert_ids_keys, expert_ids_turns).reshape((TOKENS, TOPK))
    route_weights = jnp.clip(0.02 + 0.28 * jax.random.uniform(own_keys[3], (TOKENS, TOPK), jnp.float32) ** steps_of(own_keys[3], (TOKENS, TOPK), ((0, 16),), -0.2, 0.2), 0.02, 0.3)
    w_gate = normal_values(key_list[4], (EXPERTS, FF, D), D ** -0.5, 0.1875, ((0, 16),))
    w_up = normal_values(key_list[5], (EXPERTS, FF, D), D ** -0.5, 0.1875, ((0, 16),))
    w_down = normal_values(key_list[6], (EXPERTS, FF, D), FF ** -0.5, 0.3125, ((0, 16),))
    return dict(student_input=student_input, judge_output=judge_output, expert_ids=expert_ids, route_weights=route_weights, w_gate=w_gate, w_up=w_up, w_down=w_down)


def tables(ids_block, experts, capacity):
    flat_ids = ids_block.reshape(-1).astype(jnp.int32)
    pick_total = flat_ids.shape[0]
    onehot = (flat_ids[:, None] == jnp.arange(experts, dtype=jnp.int32)[None, :]).astype(jnp.int32)
    earlier = jnp.cumsum(onehot, axis=0) - onehot
    slot_index = jnp.sum(earlier * onehot, axis=1).astype(jnp.int32)
    position = (flat_ids * capacity + slot_index).astype(jnp.int32)
    source = jnp.zeros((experts * capacity,), jnp.int32).at[position].set(jnp.arange(1, pick_total + 1, dtype=jnp.int32))
    return position, source


def hidden_units(row_block, gate_w, up_w):
    gate_pre = jnp.dot(row_block, gate_w.T, preferred_element_type=jnp.float32)
    up_pre = jnp.dot(row_block, up_w.T, preferred_element_type=jnp.float32)
    hidden = (gate_pre * jax.nn.sigmoid(gate_pre) * up_pre).astype(jnp.bfloat16)
    return gate_pre, up_pre, hidden


def group_sum(left, right):
    partial_sums = jnp.einsum("gsf,gsd->gfd", left.astype(jnp.float32), right.astype(jnp.float32), precision=lax.Precision.HIGHEST)
    rounded = lax.optimization_barrier(partial_sums.astype(jnp.bfloat16))
    return jnp.sum(rounded.astype(jnp.float32), axis=0).astype(jnp.bfloat16)


def reference(student_input, judge_output, expert_ids, route_weights, w_gate, w_up, w_down):
    blocks = N_DP * N_EXPERT
    pick_total = TOK_DEV * TOPK
    ids_blocks = expert_ids.reshape(blocks, TOK_DEV, TOPK)

    def block_tables(ids_block):
        return tables(ids_block, EXPERTS, MOST)

    unused, source = jax.vmap(block_tables)(ids_blocks)
    is_live = source > 0
    offset = (jnp.arange(blocks, dtype=jnp.int32) * pick_total)[:, None]
    chosen = jnp.where(is_live, source - 1 + offset, 0).astype(jnp.int32)
    chosen = chosen.reshape(blocks, EXPERTS, MOST).transpose(1, 0, 2).reshape(EXPERTS, blocks * MOST)
    is_live = is_live.reshape(blocks, EXPERTS, MOST).transpose(1, 0, 2).reshape(EXPERTS, blocks * MOST)
    weights_flat = route_weights.reshape(-1)
    empty_rows = jnp.zeros((), jnp.bfloat16)

    def expert_pass(chosen_e, live_e, gate_w, up_w, down_w):
        token_index = (chosen_e // TOPK).astype(jnp.int32)
        row_block = jnp.where(live_e[:, None], student_input[token_index], empty_rows)
        gate_pre, up_pre, hidden = hidden_units(row_block, gate_w, up_w)
        expert_out = jnp.dot(hidden, down_w, preferred_element_type=jnp.float32).astype(jnp.bfloat16)
        weight = jnp.where(live_e, weights_flat[chosen_e], jnp.float32(0.0))
        return token_index, row_block, gate_pre, up_pre, hidden, expert_out, weight

    def forward_step(mixture, inputs):
        chosen_e, live_e, gate_w, up_w, down_w = inputs
        token_index, row_block, gate_pre, up_pre, hidden, expert_out, weight = expert_pass(chosen_e, live_e, gate_w, up_w, down_w)
        mixture = mixture.at[token_index].add(weight[:, None] * expert_out.astype(jnp.float32))
        return mixture, None

    mixture, unused_ys = lax.scan(forward_step, jnp.zeros((TOKENS, D), jnp.float32), (chosen, is_live, w_gate, w_up, w_down))
    residual = mixture - judge_output.astype(jnp.float32)

    def backward_step(route_grads, inputs):
        chosen_e, live_e, gate_w, up_w, down_w = inputs
        token_index, row_block, gate_pre, up_pre, hidden, expert_out, weight = expert_pass(chosen_e, live_e, gate_w, up_w, down_w)
        residual_rows = residual[token_index]
        inner = jnp.sum(expert_out.astype(jnp.float32) * residual_rows, axis=1)
        route_grads = route_grads.at[chosen_e].add(jnp.where(live_e, inner, jnp.float32(0.0)))
        out_grad = (weight[:, None] * residual_rows).astype(jnp.bfloat16)
        hidden_grad = jnp.dot(out_grad, down_w.T, preferred_element_type=jnp.float32)
        sig_gate = jax.nn.sigmoid(gate_pre)
        gate_grad = (hidden_grad * up_pre * sig_gate * (1.0 + gate_pre * (1.0 - sig_gate))).astype(jnp.bfloat16)
        up_grad = (hidden_grad * gate_pre * sig_gate).astype(jnp.bfloat16)
        span = N_EXPERT * MOST
        rows_grouped = row_block.reshape(N_DP, span, D)
        grad_gate_e = group_sum(gate_grad.reshape(N_DP, span, FF), rows_grouped)
        grad_up_e = group_sum(up_grad.reshape(N_DP, span, FF), rows_grouped)
        grad_down_e = group_sum(hidden.reshape(N_DP, span, FF), out_grad.reshape(N_DP, span, D))
        return route_grads, (grad_gate_e, grad_up_e, grad_down_e)

    route_grads, grads = lax.scan(backward_step, jnp.zeros((TOKENS * TOPK,), jnp.float32), (chosen, is_live, w_gate, w_up, w_down))
    return (mixture.astype(jnp.bfloat16), route_grads.reshape(TOKENS, TOPK), grads[0], grads[1], grads[2])
```

```python
import math

import jax
import jax.numpy as jnp
from jax import lax
from jax.sharding import PartitionSpec as P


def slot_layout(flat_ids, experts, capacity):
    pick_total = flat_ids.shape[0]
    span = math.gcd(pick_total, 128)
    count_blocks = pick_total // span
    onehot = (flat_ids[:, None] == jnp.arange(experts, dtype=jnp.int32)[None, :]).astype(
        jnp.bfloat16
    )
    onehot = onehot.reshape(count_blocks, span, experts)
    rows_here = jnp.arange(span, dtype=jnp.int32)
    lower = (rows_here[:, None] > rows_here[None, :]).astype(jnp.bfloat16)
    within = jnp.einsum("ij,bje->bie", lower, onehot, preferred_element_type=jnp.float32)
    totals = jnp.sum(onehot.astype(jnp.float32), axis=1)
    before = jnp.cumsum(totals, axis=0) - totals
    earlier = within + before[:, None, :]
    slot_index = jnp.sum(earlier * onehot.astype(jnp.float32), axis=2).reshape(-1).astype(jnp.int32)
    position = flat_ids * capacity + slot_index
    source = (
        jnp.zeros((experts * capacity,), jnp.int32)
        .at[position]
        .set(jnp.arange(1, pick_total + 1, dtype=jnp.int32))
    )
    return (position, source)


def hidden_units(row_block, gate_full, up_full):
    gate_pre = jnp.einsum("esd,efd->esf", row_block, gate_full, preferred_element_type=jnp.float32)
    up_pre = jnp.einsum("esd,efd->esf", row_block, up_full, preferred_element_type=jnp.float32)
    hidden = (gate_pre * jax.nn.sigmoid(gate_pre) * up_pre).astype(jnp.bfloat16)
    return (gate_pre, up_pre, hidden)


def routed_rows(student_input, judge_output, expert_ids, route_weights, w_gate, w_up, w_down):
    tok_count, dim_model = student_input.shape
    top_picks = expert_ids.shape[1]
    exp_local = w_gate.shape[0]
    senders = lax.axis_size("expert")
    experts = exp_local * senders
    capacity = min(tok_count, tok_count * top_picks * 5 // (4 * experts))
    flat_ids = expert_ids.reshape(-1)
    position, source = slot_layout(flat_ids, experts, capacity)
    is_valid = (source > 0)[:, None]
    pick_index = jnp.maximum(source - 1, 0)
    empty_rows = jnp.zeros((), jnp.bfloat16)
    send_rows = jnp.where(is_valid, student_input[pick_index // top_picks], empty_rows).reshape(
        experts, capacity, dim_model
    )
    gate_full, up_full, down_full = (
        lax.all_gather(w_gate, "dp", axis=1, tiled=True),
        lax.all_gather(w_up, "dp", axis=1, tiled=True),
        lax.all_gather(w_down, "dp", axis=1, tiled=True),
    )
    row_block = lax.all_to_all(send_rows, "expert", split_axis=0, concat_axis=1, tiled=True)
    gate_pre, up_pre, hidden = hidden_units(row_block, gate_full, up_full)
    expert_out = jnp.einsum(
        "esf,efd->esd", hidden, down_full, preferred_element_type=jnp.float32
    ).astype(jnp.bfloat16)
    returned = lax.all_to_all(
        expert_out, "expert", split_axis=1, concat_axis=0, tiled=True
    ).reshape(experts * capacity, dim_model)
    pick_out = returned[position].reshape(tok_count, top_picks, dim_model)
    pick_wide = pick_out.astype(jnp.float32)
    mixture = jnp.sum(route_weights[:, :, None] * pick_wide, axis=1)
    residual = mixture - judge_output.astype(jnp.float32)
    route_grads = jnp.sum(pick_wide * residual[:, None, :], axis=2)
    out_grad = (
        (route_weights[:, :, None] * residual[:, None, :])
        .astype(jnp.bfloat16)
        .reshape(tok_count * top_picks, dim_model)
    )
    send_grads = jnp.where(is_valid, out_grad[pick_index], empty_rows).reshape(
        experts, capacity, dim_model
    )
    grad_block = lax.all_to_all(send_grads, "expert", split_axis=0, concat_axis=1, tiled=True)
    hidden_grad = jnp.einsum(
        "esd,efd->esf", grad_block, down_full, preferred_element_type=jnp.float32
    )
    sig_gate = jax.nn.sigmoid(gate_pre)
    gate_grad = (hidden_grad * up_pre * sig_gate * (1.0 + gate_pre * (1.0 - sig_gate))).astype(
        jnp.bfloat16
    )
    up_grad = (hidden_grad * gate_pre * sig_gate).astype(jnp.bfloat16)
    gate_part = jnp.einsum("esf,esd->efd", gate_grad, row_block, preferred_element_type=jnp.float32)
    up_part = jnp.einsum("esf,esd->efd", up_grad, row_block, preferred_element_type=jnp.float32)
    down_part = jnp.einsum("esf,esd->efd", hidden, grad_block, preferred_element_type=jnp.float32)
    grad_gate, grad_up, grad_down = (
        lax.psum_scatter(
            gate_part.astype(jnp.bfloat16), "dp", scatter_dimension=1, tiled=True
        ).astype(jnp.float32),
        lax.psum_scatter(
            up_part.astype(jnp.bfloat16), "dp", scatter_dimension=1, tiled=True
        ).astype(jnp.float32),
        lax.psum_scatter(
            down_part.astype(jnp.bfloat16), "dp", scatter_dimension=1, tiled=True
        ).astype(jnp.float32),
    )
    return (
        mixture.astype(jnp.bfloat16),
        route_grads,
        grad_gate.astype(jnp.bfloat16),
        grad_up.astype(jnp.bfloat16),
        grad_down.astype(jnp.bfloat16),
    )


def dense_rows(student_input, judge_output, expert_ids, route_weights, w_gate, w_up, w_down):
    senders = lax.axis_size("expert")
    exp_local = w_gate.shape[0]
    experts = exp_local * senders
    tok_count, dim_model = student_input.shape
    gate_full, up_full, down_full = (
        lax.all_gather(w_gate, "dp", axis=1, tiled=True),
        lax.all_gather(w_up, "dp", axis=1, tiled=True),
        lax.all_gather(w_down, "dp", axis=1, tiled=True),
    )
    chosen = expert_ids[:, :, None] == jnp.arange(experts, dtype=jnp.int32)[None, None, :]
    dense_weights = jnp.sum(jnp.where(chosen, route_weights[:, :, None], 0.0), axis=1)
    rows = lax.all_gather(student_input, "expert", axis=0, tiled=True)
    weights_here = lax.all_to_all(
        dense_weights.T.reshape(senders, exp_local, tok_count),
        "expert",
        split_axis=0,
        concat_axis=0,
        tiled=True,
    )
    weights_here = weights_here.transpose(1, 0, 2).reshape(exp_local, senders * tok_count, 1)
    gate_pre = jnp.einsum("sd,efd->esf", rows, gate_full, preferred_element_type=jnp.float32)
    up_pre = jnp.einsum("sd,efd->esf", rows, up_full, preferred_element_type=jnp.float32)
    sig_gate = jax.nn.sigmoid(gate_pre)
    hidden = (gate_pre * sig_gate * up_pre).astype(jnp.bfloat16)
    expert_out = jnp.einsum(
        "esf,efd->esd", hidden, down_full, preferred_element_type=jnp.float32
    ).astype(jnp.bfloat16)
    weighted = jnp.sum(weights_here * expert_out.astype(jnp.float32), axis=0).astype(jnp.bfloat16)
    mixture = lax.psum_scatter(weighted, "expert", scatter_dimension=0, tiled=True)
    residual = (mixture.astype(jnp.float32) - judge_output.astype(jnp.float32)).astype(jnp.bfloat16)
    residual_rows = lax.all_gather(residual, "expert", axis=0, tiled=True).astype(jnp.float32)
    inner = jnp.sum(expert_out.astype(jnp.float32) * residual_rows[None], axis=2)
    inner_back = lax.all_to_all(
        inner.reshape(exp_local, senders, tok_count).transpose(1, 0, 2),
        "expert",
        split_axis=0,
        concat_axis=0,
        tiled=True,
    ).reshape(experts, tok_count)
    route_grads = jnp.sum(jnp.where(chosen, inner_back.T[:, None, :], 0.0), axis=2)
    out_grad = (weights_here * residual_rows[None]).astype(jnp.bfloat16)
    hidden_grad = jnp.einsum("esd,efd->esf", out_grad, down_full, preferred_element_type=jnp.float32)
    gate_grad = (hidden_grad * up_pre * sig_gate * (1.0 + gate_pre * (1.0 - sig_gate))).astype(
        jnp.bfloat16
    )
    up_grad = (hidden_grad * gate_pre * sig_gate).astype(jnp.bfloat16)
    parts = (
        jnp.einsum("esf,sd->efd", gate_grad, rows, preferred_element_type=jnp.float32),
        jnp.einsum("esf,sd->efd", up_grad, rows, preferred_element_type=jnp.float32),
        jnp.einsum("esf,esd->efd", hidden, out_grad, preferred_element_type=jnp.float32),
    )
    grads = [
        lax.psum_scatter(part.astype(jnp.bfloat16), "dp", scatter_dimension=1, tiled=True)
        for part in parts
    ]
    return (mixture, route_grads, *grads)


def on_device(student_input, judge_output, expert_ids, route_weights, w_gate, w_up, w_down):
    experts = w_gate.shape[0] * lax.axis_size("expert")
    form = dense_rows if experts <= 4 * expert_ids.shape[1] else routed_rows
    return form(student_input, judge_output, expert_ids, route_weights, w_gate, w_up, w_down)


def solution(mesh):
    placed = (
        P(("groups", "dp", "expert"), None),
        P(("groups", "dp", "expert"), None),
        P(("groups", "dp", "expert"), None),
        P(("groups", "dp", "expert"), None),
        P("expert", "dp", None),
        P("expert", "dp", None),
        P("expert", "dp", None),
    )
    return jax.shard_map(
        on_device,
        mesh=mesh,
        in_specs=placed,
        out_specs=(
            P(("groups", "dp", "expert"), None),
            P(("groups", "dp", "expert"), None),
            P(("groups", "expert"), "dp", None),
            P(("groups", "expert"), "dp", None),
            P(("groups", "expert"), "dp", None),
        ),
        check_vma=False,
    )
```

```python
import functools
import math

import jax
import jax.numpy as jnp
from jax import lax
from jax.experimental import pallas as pl
from jax.experimental.pallas import tpu as pltpu
from jax.sharding import PartitionSpec as P


def slot_layout(flat_ids, experts, capacity):
    pick_total = flat_ids.shape[0]
    span = math.gcd(pick_total, 128)
    count_blocks = pick_total // span
    onehot = (flat_ids[:, None] == jnp.arange(experts, dtype=jnp.int32)[None, :]).astype(
        jnp.bfloat16
    )
    onehot = onehot.reshape(count_blocks, span, experts)
    rows_here = jnp.arange(span, dtype=jnp.int32)
    lower = (rows_here[:, None] > rows_here[None, :]).astype(jnp.bfloat16)
    within = jnp.einsum("ij,bje->bie", lower, onehot, preferred_element_type=jnp.float32)
    totals = jnp.sum(onehot.astype(jnp.float32), axis=1)
    before = jnp.cumsum(totals, axis=0) - totals
    earlier = within + before[:, None, :]
    slot_index = jnp.sum(earlier * onehot.astype(jnp.float32), axis=2).reshape(-1).astype(jnp.int32)
    position = flat_ids * capacity + slot_index
    source = (
        jnp.zeros((experts * capacity,), jnp.int32)
        .at[position]
        .set(jnp.arange(1, pick_total + 1, dtype=jnp.int32))
    )
    return (position, source)


def hidden_units(row_block, gate_full, up_full):
    gate_pre = jnp.einsum("esd,efd->esf", row_block, gate_full, preferred_element_type=jnp.float32)
    up_pre = jnp.einsum("esd,efd->esf", row_block, up_full, preferred_element_type=jnp.float32)
    hidden = (gate_pre * jax.nn.sigmoid(gate_pre) * up_pre).astype(jnp.bfloat16)
    return (gate_pre, up_pre, hidden)


def routed_rows(student_input, judge_output, expert_ids, route_weights, w_gate, w_up, w_down):
    tok_count, dim_model = student_input.shape
    top_picks = expert_ids.shape[1]
    exp_local = w_gate.shape[0]
    senders = lax.axis_size("expert")
    experts = exp_local * senders
    capacity = min(tok_count, tok_count * top_picks * 5 // (4 * experts))
    flat_ids = expert_ids.reshape(-1)
    position, source = slot_layout(flat_ids, experts, capacity)
    is_valid = (source > 0)[:, None]
    pick_index = jnp.maximum(source - 1, 0)
    empty_rows = jnp.zeros((), jnp.bfloat16)
    send_rows = jnp.where(is_valid, student_input[pick_index // top_picks], empty_rows).reshape(
        experts, capacity, dim_model
    )
    gate_full, up_full, down_full = (
        lax.all_gather(w_gate, "dp", axis=1, tiled=True),
        lax.all_gather(w_up, "dp", axis=1, tiled=True),
        lax.all_gather(w_down, "dp", axis=1, tiled=True),
    )
    row_block = lax.all_to_all(send_rows, "expert", split_axis=0, concat_axis=1, tiled=True)
    gate_pre, up_pre, hidden = hidden_units(row_block, gate_full, up_full)
    expert_out = jnp.einsum(
        "esf,efd->esd", hidden, down_full, preferred_element_type=jnp.float32
    ).astype(jnp.bfloat16)
    returned = lax.all_to_all(
        expert_out, "expert", split_axis=1, concat_axis=0, tiled=True
    ).reshape(experts * capacity, dim_model)
    pick_out = returned[position].reshape(tok_count, top_picks, dim_model)
    pick_wide = pick_out.astype(jnp.float32)
    mixture = jnp.sum(route_weights[:, :, None] * pick_wide, axis=1)
    residual = mixture - judge_output.astype(jnp.float32)
    route_grads = jnp.sum(pick_wide * residual[:, None, :], axis=2)
    out_grad = (
        (route_weights[:, :, None] * residual[:, None, :])
        .astype(jnp.bfloat16)
        .reshape(tok_count * top_picks, dim_model)
    )
    send_grads = jnp.where(is_valid, out_grad[pick_index], empty_rows).reshape(
        experts, capacity, dim_model
    )
    grad_block = lax.all_to_all(send_grads, "expert", split_axis=0, concat_axis=1, tiled=True)
    hidden_grad = jnp.einsum(
        "esd,efd->esf", grad_block, down_full, preferred_element_type=jnp.float32
    )
    sig_gate = jax.nn.sigmoid(gate_pre)
    gate_grad = (hidden_grad * up_pre * sig_gate * (1.0 + gate_pre * (1.0 - sig_gate))).astype(
        jnp.bfloat16
    )
    up_grad = (hidden_grad * gate_pre * sig_gate).astype(jnp.bfloat16)
    gate_part = jnp.einsum("esf,esd->efd", gate_grad, row_block, preferred_element_type=jnp.float32)
    up_part = jnp.einsum("esf,esd->efd", up_grad, row_block, preferred_element_type=jnp.float32)
    down_part = jnp.einsum("esf,esd->efd", hidden, grad_block, preferred_element_type=jnp.float32)
    grad_gate, grad_up, grad_down = (
        lax.psum_scatter(
            gate_part.astype(jnp.bfloat16), "dp", scatter_dimension=1, tiled=True
        ).astype(jnp.float32),
        lax.psum_scatter(
            up_part.astype(jnp.bfloat16), "dp", scatter_dimension=1, tiled=True
        ).astype(jnp.float32),
        lax.psum_scatter(
            down_part.astype(jnp.bfloat16), "dp", scatter_dimension=1, tiled=True
        ).astype(jnp.float32),
    )
    return (
        mixture.astype(jnp.bfloat16),
        route_grads,
        grad_gate.astype(jnp.bfloat16),
        grad_up.astype(jnp.bfloat16),
        grad_down.astype(jnp.bfloat16),
    )


UP, DOWN, ACROSS, SIBLING = range(4)
MESH = pl.DeviceIdType.MESH


def place(senders):
    me = lax.axis_index("expert")
    depth = senders // 4
    z, x, c = me // 4, (me // 2) % 2, me % 2
    return depth, z, x, c


def index_of(z, x, c):
    return z * 4 + x * 2 + c


def remote(src, dst, send_sem, recv_sem, device):
    return pltpu.make_async_remote_copy(
        src_ref=src,
        dst_ref=dst,
        send_sem=send_sem,
        recv_sem=recv_sem,
        device_id={"expert": device},
        device_id_type=MESH,
    )


def greet_all(senders):
    me = lax.axis_index("expert")
    barrier = pltpu.get_barrier_semaphore()
    for step in range(1, senders):
        other = lax.rem(me + step, senders)
        pl.semaphore_signal(barrier, inc=1, device_id={"expert": other}, device_id_type=MESH)
    pl.semaphore_wait(barrier, senders - 1)


def gather_blocks(senders, out, send_sem, recv_sem):
    depth, z, x, c = place(senders)
    targets = {
        UP: lambda: index_of(z + 1, x, c),
        DOWN: lambda: index_of(z - 1, x, c),
        ACROSS: lambda: index_of(z, 1 - x, c),
        SIBLING: lambda: index_of(z, x, 1 - c),
    }

    def copy(slot, way):
        return remote(
            out.at[slot], out.at[slot], send_sem.at[slot, way], recv_sem.at[slot], targets[way]()
        )

    def each_column_copy(act):
        own = index_of(z, x, c)
        pl.when(z < depth - 1)(lambda: act(own, UP, None))
        pl.when(z > 0)(lambda: act(own, DOWN, None))
        act(own, ACROSS, None)
        act(own, SIBLING, None)
        for d in range(1, depth):
            from_below, from_above = index_of(z - d, x, c), index_of(z + d, x, c)

            @pl.when(z - d >= 0)
            def _():
                act(None, None, from_below)
                pl.when(z < depth - 1)(lambda: act(from_below, UP, None))
                act(from_below, ACROSS, None)
                act(from_below, SIBLING, None)

            @pl.when(z + d < depth)
            def _():
                act(None, None, from_above)
                pl.when(z > 0)(lambda: act(from_above, DOWN, None))
                act(from_above, ACROSS, None)
                act(from_above, SIBLING, None)

    def arrive_or_start(slot, way, arrival):
        if arrival is None:
            copy(slot, way).start()
        else:
            copy(arrival, ACROSS).wait_recv()

    def finish(slot, way, arrival):
        if arrival is None:
            copy(slot, way).wait_send()

    def across_order():
        yield z, None
        for d in range(1, depth):
            yield z - d, z - d >= 0
            yield z + d, z + d < depth

    each_column_copy(arrive_or_start)
    for zb, here in across_order():

        def pass_on(zb=zb):
            slot = index_of(zb, 1 - x, c)
            copy(slot, ACROSS).wait_recv()
            copy(slot, SIBLING).start()

        pass_on() if here is None else pl.when(here)(pass_on)
    for zb in range(depth):
        for xb in range(2):
            copy(index_of(zb, xb, 1 - c), ACROSS).wait_recv()
    each_column_copy(finish)
    for zb in range(depth):
        copy(index_of(zb, 1 - x, c), SIBLING).wait_send()


def spread_kernel(
    senders, row_ref, weight_ref, out, weight_out, send_sem, recv_sem, weight_send, weight_recv
):
    me = lax.axis_index("expert")
    out[me] = row_ref[...]
    weight_out[me] = weight_ref[me]
    greet_all(senders)

    def weight_copy(step):
        other = lax.rem(me + step, senders)
        return remote(
            weight_ref.at[other],
            weight_out.at[me],
            weight_send.at[other],
            weight_recv.at[me],
            other,
        )

    def weight_arrival(step):
        other = lax.rem(me + step, senders)
        return remote(
            weight_ref.at[other],
            weight_out.at[other],
            weight_send.at[other],
            weight_recv.at[other],
            other,
        )

    for step in range(1, senders):
        weight_copy(step).start()
    gather_blocks(senders, out, send_sem, recv_sem)
    for step in range(1, senders):
        weight_arrival(step).wait_recv()
        weight_copy(step).wait_send()


def mix_kernel(
    senders,
    part_ref,
    judge_ref,
    mixture_ref,
    out,
    sib_in,
    x_out,
    x_in,
    z_out,
    up_in,
    down_in,
    out_total,
    sib_send,
    sib_recv,
    x_send,
    x_recv,
    z_send,
    up_recv,
    down_recv,
    send_sem,
    recv_sem,
):
    depth, z, x, c = place(senders)
    greet_all(senders)

    def by_distance(act):
        for d in range(depth - 1, 0, -1):
            pl.when(z + d < depth)(functools.partial(act, z + d, UP))
            pl.when(z - d >= 0)(functools.partial(act, z - d, DOWN))
        act(z, None)

    def sib_copy(zb, xb):
        slot = zb * 2 + xb
        return remote(
            part_ref.at[index_of(zb, xb, 1 - c)],
            sib_in.at[slot],
            sib_send.at[slot],
            sib_recv.at[slot],
            index_of(z, x, 1 - c),
        )

    def x_copy(zb):
        return remote(
            x_out.at[zb], x_in.at[zb], x_send.at[zb], x_recv.at[zb], index_of(z, 1 - x, c)
        )

    def up_copy(zb):
        return remote(
            z_out.at[zb], up_in.at[zb], z_send.at[zb], up_recv.at[zb], index_of(z + 1, x, c)
        )

    def down_copy(zb):
        return remote(
            z_out.at[zb], down_in.at[zb], z_send.at[zb], down_recv.at[zb], index_of(z - 1, x, c)
        )

    def start_sibling(zb, way):
        sib_copy(zb, 1 - x).start()
        sib_copy(zb, x).start()

    def pair_sum(zb, xb):
        sib_copy(zb, xb).wait_recv()
        mine = part_ref[index_of(zb, xb, c)].astype(jnp.float32)
        return mine + sib_in[zb * 2 + xb].astype(jnp.float32)

    def send_across(zb, way):
        x_out[zb] = pair_sum(zb, 1 - x).astype(jnp.bfloat16)
        x_copy(zb).start()

    def chip_sum(zb):
        total = pair_sum(zb, x)
        x_copy(zb).wait_recv()
        return total + x_in[zb].astype(jnp.float32)

    def send_along(zb, way):
        total = chip_sum(zb)
        if way is None:
            out_total[...] = total

            @pl.when(z > 0)
            def _():
                up_copy(zb).wait_recv()
                out_total[...] += up_in[zb].astype(jnp.float32)

            @pl.when(z < depth - 1)
            def _():
                down_copy(zb).wait_recv()
                out_total[...] += down_in[zb].astype(jnp.float32)

            return
        z_out[zb] = total.astype(jnp.bfloat16)
        step_copy, landed, here = (
            (up_copy, up_in, z > 0) if way == UP else (down_copy, down_in, z < depth - 1)
        )

        @pl.when(here)
        def _():
            step_copy(zb).wait_recv()
            more = pair_again(zb) + landed[zb].astype(jnp.float32)
            z_out[zb] = more.astype(jnp.bfloat16)

        step_copy(zb).start()

    def pair_again(zb):
        mine = part_ref[index_of(zb, x, c)].astype(jnp.float32)
        return mine + sib_in[zb * 2 + x].astype(jnp.float32) + x_in[zb].astype(jnp.float32)

    def finish(zb, way):
        sib_copy(zb, 1 - x).wait_send()
        sib_copy(zb, x).wait_send()
        x_copy(zb).wait_send()
        if way is not None:
            (up_copy if way == UP else down_copy)(zb).wait_send()

    by_distance(start_sibling)
    by_distance(send_across)
    by_distance(send_along)
    mixture = out_total[...]
    mixture_ref[...] = mixture.astype(jnp.bfloat16)
    out[index_of(z, x, c)] = (mixture - judge_ref[...].astype(jnp.float32)).astype(jnp.bfloat16)
    gather_blocks(senders, out, send_sem, recv_sem)
    by_distance(finish)


def vmem_specs(count):
    return [pl.BlockSpec(memory_space=pltpu.VMEM)] * count


def spread_rows(rows, weights):
    senders = weights.shape[0]
    dma = pltpu.SemaphoreType.DMA
    return pl.pallas_call(
        functools.partial(spread_kernel, senders),
        out_shape=(
            jax.ShapeDtypeStruct((senders, *rows.shape), rows.dtype),
            jax.ShapeDtypeStruct(weights.shape, weights.dtype),
        ),
        in_specs=vmem_specs(2),
        out_specs=tuple(vmem_specs(2)),
        scratch_shapes=[dma((senders, 4)), dma((senders,)), dma((senders,)), dma((senders,))],
        compiler_params=pltpu.CompilerParams(
            collective_id=0, has_side_effects=True, vmem_limit_bytes=16 << 20
        ),
    )(rows, weights)


def mix_rows(parts, judge):
    senders = parts.shape[0]
    depth = senders // 4
    block = judge.shape
    dma = pltpu.SemaphoreType.DMA

    def blocks(count):
        return pltpu.VMEM((count, *block), jnp.bfloat16)

    return pl.pallas_call(
        functools.partial(mix_kernel, senders),
        out_shape=(
            jax.ShapeDtypeStruct(block, jnp.bfloat16),
            jax.ShapeDtypeStruct((senders, *block), jnp.bfloat16),
        ),
        in_specs=vmem_specs(2),
        out_specs=tuple(vmem_specs(2)),
        scratch_shapes=[
            blocks(2 * depth),
            blocks(depth),
            blocks(depth),
            blocks(depth),
            blocks(depth),
            blocks(depth),
            pltpu.VMEM(block, jnp.float32),
            dma((2 * depth,)),
            dma((2 * depth,)),
            dma((depth,)),
            dma((depth,)),
            dma((depth,)),
            dma((depth,)),
            dma((depth,)),
            dma((senders, 4)),
            dma((senders,)),
        ],
        compiler_params=pltpu.CompilerParams(
            collective_id=1, has_side_effects=True, vmem_limit_bytes=32 << 20
        ),
    )(parts, judge)


def dense_rows(student_input, judge_output, expert_ids, route_weights, w_gate, w_up, w_down):
    senders = lax.axis_size("expert")
    exp_local = w_gate.shape[0]
    experts = exp_local * senders
    tok_count, dim_model = student_input.shape
    gate_full, up_full, down_full = (
        lax.all_gather(w_gate, "dp", axis=1, tiled=True),
        lax.all_gather(w_up, "dp", axis=1, tiled=True),
        lax.all_gather(w_down, "dp", axis=1, tiled=True),
    )
    chosen = expert_ids[:, :, None] == jnp.arange(experts, dtype=jnp.int32)[None, None, :]
    dense_weights = jnp.sum(jnp.where(chosen, route_weights[:, :, None], 0.0), axis=1)
    by_expert = dense_weights.T.reshape(senders, exp_local, tok_count)
    padded = jnp.pad(by_expert, ((0, 0), (0, -exp_local % 8), (0, 0)))
    rows, weights_here = spread_rows(student_input, padded)
    rows = rows.reshape(senders * tok_count, dim_model)
    weights_here = weights_here[:, :exp_local].transpose(1, 0, 2)
    weights_here = weights_here.reshape(exp_local, senders * tok_count, 1)
    gate_pre = jnp.einsum("sd,efd->esf", rows, gate_full, preferred_element_type=jnp.float32)
    up_pre = jnp.einsum("sd,efd->esf", rows, up_full, preferred_element_type=jnp.float32)
    sig_gate = jax.nn.sigmoid(gate_pre)
    hidden = (gate_pre * sig_gate * up_pre).astype(jnp.bfloat16)
    expert_out = jnp.einsum(
        "esf,efd->esd", hidden, down_full, preferred_element_type=jnp.float32
    ).astype(jnp.bfloat16)
    weighted = jnp.sum(weights_here * expert_out.astype(jnp.float32), axis=0).astype(jnp.bfloat16)
    mixture, residual_rows = mix_rows(weighted.reshape(senders, tok_count, dim_model), judge_output)
    residual_rows = residual_rows.reshape(senders * tok_count, dim_model).astype(jnp.float32)
    inner = jnp.sum(expert_out.astype(jnp.float32) * residual_rows[None], axis=2)
    inner_back = lax.all_to_all(
        inner.reshape(exp_local, senders, tok_count).transpose(1, 0, 2),
        "expert",
        split_axis=0,
        concat_axis=0,
        tiled=True,
    ).reshape(experts, tok_count)
    route_grads = jnp.sum(jnp.where(chosen, inner_back.T[:, None, :], 0.0), axis=2)
    out_grad = (weights_here * residual_rows[None]).astype(jnp.bfloat16)
    hidden_grad = jnp.einsum("esd,efd->esf", out_grad, down_full, preferred_element_type=jnp.float32)
    gate_grad = (hidden_grad * up_pre * sig_gate * (1.0 + gate_pre * (1.0 - sig_gate))).astype(
        jnp.bfloat16
    )
    up_grad = (hidden_grad * gate_pre * sig_gate).astype(jnp.bfloat16)
    parts = (
        jnp.einsum("esf,sd->efd", gate_grad, rows, preferred_element_type=jnp.float32),
        jnp.einsum("esf,sd->efd", up_grad, rows, preferred_element_type=jnp.float32),
        jnp.einsum("esf,esd->efd", hidden, out_grad, preferred_element_type=jnp.float32),
    )
    grads = [
        lax.psum_scatter(part.astype(jnp.bfloat16), "dp", scatter_dimension=1, tiled=True)
        for part in parts
    ]
    return (mixture, route_grads, *grads)


def on_device(student_input, judge_output, expert_ids, route_weights, w_gate, w_up, w_down):
    experts = w_gate.shape[0] * lax.axis_size("expert")
    dense = experts <= 4 * expert_ids.shape[1] and lax.axis_size("expert") % 4 == 0
    form = dense_rows if dense else routed_rows
    return form(student_input, judge_output, expert_ids, route_weights, w_gate, w_up, w_down)


def solution(mesh):
    placed = (
        P(("groups", "dp", "expert"), None),
        P(("groups", "dp", "expert"), None),
        P(("groups", "dp", "expert"), None),
        P(("groups", "dp", "expert"), None),
        P("expert", "dp", None),
        P("expert", "dp", None),
        P("expert", "dp", None),
    )
    return jax.shard_map(
        on_device,
        mesh=mesh,
        in_specs=placed,
        out_specs=(
            P(("groups", "dp", "expert"), None),
            P(("groups", "dp", "expert"), None),
            P(("groups", "expert"), "dp", None),
            P(("groups", "expert"), "dp", None),
            P(("groups", "expert"), "dp", None),
        ),
        check_vma=False,
    )
```

```python
import functools
import math

import jax
import jax.numpy as jnp
from jax import lax
from jax.experimental import pallas as pl
from jax.experimental.pallas import tpu as pltpu
from jax.sharding import PartitionSpec as P


def slot_layout(flat_ids, experts, capacity):
    pick_total = flat_ids.shape[0]
    span = math.gcd(pick_total, 128)
    count_blocks = pick_total // span
    onehot = (flat_ids[:, None] == jnp.arange(experts, dtype=jnp.int32)[None, :]).astype(
        jnp.bfloat16
    )
    onehot = onehot.reshape(count_blocks, span, experts)
    rows_here = jnp.arange(span, dtype=jnp.int32)
    lower = (rows_here[:, None] > rows_here[None, :]).astype(jnp.bfloat16)
    within = jnp.einsum("ij,bje->bie", lower, onehot, preferred_element_type=jnp.float32)
    totals = jnp.sum(onehot.astype(jnp.float32), axis=1)
    before = jnp.cumsum(totals, axis=0) - totals
    earlier = within + before[:, None, :]
    slot_index = jnp.sum(earlier * onehot.astype(jnp.float32), axis=2).reshape(-1).astype(jnp.int32)
    position = flat_ids * capacity + slot_index
    source = (
        jnp.zeros((experts * capacity,), jnp.int32)
        .at[position]
        .set(jnp.arange(1, pick_total + 1, dtype=jnp.int32))
    )
    return (position, source)


def hidden_units(row_block, gate_full, up_full):
    gate_pre = jnp.einsum("esd,efd->esf", row_block, gate_full, preferred_element_type=jnp.float32)
    up_pre = jnp.einsum("esd,efd->esf", row_block, up_full, preferred_element_type=jnp.float32)
    hidden = (gate_pre * jax.nn.sigmoid(gate_pre) * up_pre).astype(jnp.bfloat16)
    return (gate_pre, up_pre, hidden)


def routed_rows(student_input, judge_output, expert_ids, route_weights, w_gate, w_up, w_down):
    tok_count, dim_model = student_input.shape
    top_picks = expert_ids.shape[1]
    exp_local = w_gate.shape[0]
    senders = lax.axis_size("expert")
    experts = exp_local * senders
    capacity = min(tok_count, tok_count * top_picks * 5 // (4 * experts))
    flat_ids = expert_ids.reshape(-1)
    position, source = slot_layout(flat_ids, experts, capacity)
    is_valid = (source > 0)[:, None]
    pick_index = jnp.maximum(source - 1, 0)
    empty_rows = jnp.zeros((), jnp.bfloat16)
    send_rows = jnp.where(is_valid, student_input[pick_index // top_picks], empty_rows).reshape(
        experts, capacity, dim_model
    )
    gate_full, up_full, down_full = (
        lax.all_gather(w_gate, "dp", axis=1, tiled=True),
        lax.all_gather(w_up, "dp", axis=1, tiled=True),
        lax.all_gather(w_down, "dp", axis=1, tiled=True),
    )
    row_block = lax.all_to_all(send_rows, "expert", split_axis=0, concat_axis=1, tiled=True)
    gate_pre, up_pre, hidden = hidden_units(row_block, gate_full, up_full)
    expert_out = jnp.einsum(
        "esf,efd->esd", hidden, down_full, preferred_element_type=jnp.float32
    ).astype(jnp.bfloat16)
    returned = lax.all_to_all(
        expert_out, "expert", split_axis=1, concat_axis=0, tiled=True
    ).reshape(experts * capacity, dim_model)
    pick_out = returned[position].reshape(tok_count, top_picks, dim_model)
    pick_wide = pick_out.astype(jnp.float32)
    mixture = jnp.sum(route_weights[:, :, None] * pick_wide, axis=1)
    residual = mixture - judge_output.astype(jnp.float32)
    route_grads = jnp.sum(pick_wide * residual[:, None, :], axis=2)
    out_grad = (
        (route_weights[:, :, None] * residual[:, None, :])
        .astype(jnp.bfloat16)
        .reshape(tok_count * top_picks, dim_model)
    )
    send_grads = jnp.where(is_valid, out_grad[pick_index], empty_rows).reshape(
        experts, capacity, dim_model
    )
    grad_block = lax.all_to_all(send_grads, "expert", split_axis=0, concat_axis=1, tiled=True)
    hidden_grad = jnp.einsum(
        "esd,efd->esf", grad_block, down_full, preferred_element_type=jnp.float32
    )
    sig_gate = jax.nn.sigmoid(gate_pre)
    gate_grad = (hidden_grad * up_pre * sig_gate * (1.0 + gate_pre * (1.0 - sig_gate))).astype(
        jnp.bfloat16
    )
    up_grad = (hidden_grad * gate_pre * sig_gate).astype(jnp.bfloat16)
    gate_part = jnp.einsum("esf,esd->efd", gate_grad, row_block, preferred_element_type=jnp.float32)
    up_part = jnp.einsum("esf,esd->efd", up_grad, row_block, preferred_element_type=jnp.float32)
    down_part = jnp.einsum("esf,esd->efd", hidden, grad_block, preferred_element_type=jnp.float32)
    grad_gate, grad_up, grad_down = (
        lax.psum_scatter(
            gate_part.astype(jnp.bfloat16), "dp", scatter_dimension=1, tiled=True
        ).astype(jnp.float32),
        lax.psum_scatter(
            up_part.astype(jnp.bfloat16), "dp", scatter_dimension=1, tiled=True
        ).astype(jnp.float32),
        lax.psum_scatter(
            down_part.astype(jnp.bfloat16), "dp", scatter_dimension=1, tiled=True
        ).astype(jnp.float32),
    )
    return (
        mixture.astype(jnp.bfloat16),
        route_grads,
        grad_gate.astype(jnp.bfloat16),
        grad_up.astype(jnp.bfloat16),
        grad_down.astype(jnp.bfloat16),
    )


UP, DOWN, ACROSS, SIBLING = range(4)
MESH = pl.DeviceIdType.MESH


def place(senders):
    me = lax.axis_index("expert")
    depth = senders // 4
    z, x, c = me // 4, (me // 2) % 2, me % 2
    return depth, z, x, c


def index_of(z, x, c):
    return z * 4 + x * 2 + c


def remote(src, dst, send_sem, recv_sem, device):
    return pltpu.make_async_remote_copy(
        src_ref=src,
        dst_ref=dst,
        send_sem=send_sem,
        recv_sem=recv_sem,
        device_id={"expert": device},
        device_id_type=MESH,
    )


def greet_all(senders):
    me = lax.axis_index("expert")
    barrier = pltpu.get_barrier_semaphore()
    for step in range(1, senders):
        other = lax.rem(me + step, senders)
        pl.semaphore_signal(barrier, inc=1, device_id={"expert": other}, device_id_type=MESH)
    pl.semaphore_wait(barrier, senders - 1)


def gather_blocks(senders, out, send_sem, recv_sem, visit):
    depth, z, x, c = place(senders)
    targets = {
        UP: lambda: index_of(z + 1, x, c),
        DOWN: lambda: index_of(z - 1, x, c),
        ACROSS: lambda: index_of(z, 1 - x, c),
        SIBLING: lambda: index_of(z, x, 1 - c),
    }

    def copy(slot, way):
        return remote(
            out.at[slot], out.at[slot], send_sem.at[slot, way], recv_sem.at[slot], targets[way]()
        )

    def arrived(slot):
        copy(slot, ACROSS).wait_recv()

    def send_on(zb, act):
        slot = index_of(zb, x, c)
        pl.when((zb <= z) & (z < depth - 1))(lambda: act(copy(slot, UP)))
        pl.when((zb >= z) & (z > 0))(lambda: act(copy(slot, DOWN)))
        act(copy(slot, ACROSS))
        act(copy(slot, SIBLING))

    def layer(q):
        return z + (q + 1) // 2 * (2 * (q % 2) - 1)

    def valid(q):
        return (layer(q) >= 0) & (layer(q) < depth) & (q < 2 * depth - 1)

    send_on(z, lambda one: one.start())

    @pl.loop(0, 2 * depth - 1)
    def _(q):
        @pl.when(valid(q + 1))
        def _():
            arrived(index_of(layer(q + 1), x, c))
            send_on(layer(q + 1), lambda one: one.start())

        @pl.when(valid(q))
        def _():
            zb = layer(q)
            slot = index_of(zb, 1 - x, c)
            arrived(slot)
            copy(slot, SIBLING).start()

            @pl.loop(0, 2)
            def _(turn):
                xb = x + turn * (1 - 2 * x)
                arrived(index_of(zb, xb, 1 - c))
                visit(zb, xb)

    @pl.loop(0, depth)
    def _(zb):
        send_on(zb, lambda one: one.wait_send())
        copy(index_of(zb, 1 - x, c), SIBLING).wait_send()


def column_of(row):
    size = row.shape[1]
    square = (size, size)
    diagonal = lax.broadcasted_iota(jnp.int32, square, 0) == lax.broadcasted_iota(
        jnp.int32, square, 1
    )
    return jnp.sum(jnp.where(diagonal, row, 0.0), axis=1, keepdims=True)


def row_of(column):
    size = column.shape[0]
    square = (size, size)
    diagonal = lax.broadcasted_iota(jnp.int32, square, 0) == lax.broadcasted_iota(
        jnp.int32, square, 1
    )
    return jnp.sum(jnp.where(diagonal, column, 0.0), axis=0, keepdims=True)


def product(left, right, left_dim, right_dim):
    return lax.dot_general(
        left, right, (((left_dim,), (right_dim,)), ((), ())), preferred_element_type=jnp.float32
    )


def layer_kernel(
    senders,
    row_ref,
    weight_ref,
    judge_ref,
    gate_ref,
    up_ref,
    down_ref,
    mixture_ref,
    inner_ref,
    grad_gate_ref,
    grad_up_ref,
    grad_down_ref,
    rows,
    weights,
    part_ref,
    expert_out,
    hidden_all,
    gate_factor,
    up_factor,
    residual,
    inner_out,
    sums,
    sib_in,
    x_out,
    x_in,
    z_out,
    up_in,
    down_in,
    out_total,
    sib_send,
    sib_recv,
    x_send,
    x_recv,
    z_send,
    up_recv,
    down_recv,
    row_send,
    row_recv,
    residual_send,
    residual_recv,
    weight_send,
    weight_recv,
    inner_send,
    inner_recv,
):
    me = lax.axis_index("expert")
    depth, z, x, c = place(senders)
    tokens, dim_model = row_ref.shape
    rows[me] = row_ref[...]
    weights[me] = weight_ref[me]
    greet_all(senders)

    def to_each(src, dst, send, recv, act):
        @pl.loop(1, senders)
        def _(step):
            other = lax.rem(me + step, senders)
            act(src, dst, send, recv, other)

    def start_one(src, dst, send, recv, other):
        remote(src.at[other], dst.at[me], send.at[other], recv.at[me], other).start()

    def land_one(src, dst, send, recv, other):
        remote(src.at[other], dst.at[other], send.at[other], recv.at[other], other).wait_recv()

    def sent_one(src, dst, send, recv, other):
        remote(src.at[other], dst.at[me], send.at[other], recv.at[me], other).wait_send()

    weight_way = (weight_ref, weights, weight_send, weight_recv)
    inner_way = (inner_out, inner_ref, inner_send, inner_recv)
    to_each(*weight_way, start_one)

    def by_distance(act):
        for d in range(depth - 1, 0, -1):
            pl.when(z + d < depth)(functools.partial(act, z + d, UP))
            pl.when(z - d >= 0)(functools.partial(act, z - d, DOWN))
        act(z, None)

    def sib_copy(zb, xb):
        slot = zb * 2 + xb
        return remote(
            part_ref.at[index_of(zb, xb, 1 - c)],
            sib_in.at[slot],
            sib_send.at[slot],
            sib_recv.at[slot],
            index_of(z, x, 1 - c),
        )

    def x_copy(zb):
        return remote(
            x_out.at[zb], x_in.at[zb], x_send.at[zb], x_recv.at[zb], index_of(z, 1 - x, c)
        )

    def up_copy(zb):
        return remote(
            z_out.at[zb], up_in.at[zb], z_send.at[zb], up_recv.at[zb], index_of(z + 1, x, c)
        )

    def down_copy(zb):
        return remote(
            z_out.at[zb], down_in.at[zb], z_send.at[zb], down_recv.at[zb], index_of(z - 1, x, c)
        )

    def pair(ref, zb, xb):
        first = index_of(zb, xb, 0)
        return jnp.concatenate([ref[first], ref[first + 1]], axis=0)

    def pair_weights(zb, xb):
        first = index_of(zb, xb, 0)
        return jnp.concatenate(
            [column_of(weights[first][:1]), column_of(weights[first + 1][:1])], axis=0
        )

    def forward(zb, xb):
        first, at = index_of(zb, xb, 0), zb * 2 + xb
        for core in range(2):

            @pl.when(first + core != me)
            def _():
                land_one(*weight_way, first + core)

        block = pair(rows, zb, xb)
        gate_pre = product(block, gate_ref[0], 1, 1)
        up_pre = product(block, up_ref[0], 1, 1)
        sig_gate = jax.nn.sigmoid(gate_pre)
        silu = gate_pre * sig_gate
        hidden = (silu * up_pre).astype(jnp.bfloat16)
        hidden_all[at] = hidden
        up_factor[at] = silu
        gate_factor[at] = up_pre * sig_gate * (1.0 + gate_pre * (1.0 - sig_gate))
        made = product(hidden, down_ref[0], 1, 0).astype(jnp.bfloat16)
        weighted = (pair_weights(zb, xb) * made.astype(jnp.float32)).astype(jnp.bfloat16)
        for core in range(2):
            expert_out[first + core] = made[core * tokens : (core + 1) * tokens]
            part_ref[first + core] = weighted[core * tokens : (core + 1) * tokens]
        sib_copy(zb, xb).start()

    def pair_sum(zb, xb):
        mine = part_ref[index_of(zb, xb, c)].astype(jnp.float32)
        return mine + sib_in[zb * 2 + xb].astype(jnp.float32)

    def send_across(zb, way):
        sib_copy(zb, 1 - x).wait_recv()
        x_out[zb] = pair_sum(zb, 1 - x).astype(jnp.bfloat16)
        x_copy(zb).start()

    def send_along(zb, way):
        sib_copy(zb, x).wait_recv()
        x_copy(zb).wait_recv()
        out_total[...] = pair_sum(zb, x) + x_in[zb].astype(jnp.float32)
        if way != DOWN:

            @pl.when(z > 0)
            def _():
                up_copy(zb).wait_recv()
                out_total[...] += up_in[zb].astype(jnp.float32)

        if way != UP:

            @pl.when(z < depth - 1)
            def _():
                down_copy(zb).wait_recv()
                out_total[...] += down_in[zb].astype(jnp.float32)

        if way is not None:
            z_out[zb] = out_total[...].astype(jnp.bfloat16)
            (up_copy if way == UP else down_copy)(zb).start()

    def finish(zb, way):
        sib_copy(zb, 1 - x).wait_send()
        sib_copy(zb, x).wait_send()
        x_copy(zb).wait_send()
        if way is not None:
            (up_copy if way == UP else down_copy)(zb).wait_send()

    def backward(zb, xb):
        first, at = index_of(zb, xb, 0), zb * 2 + xb
        wide = pair(residual, zb, xb).astype(jnp.float32)
        out_grad = (pair_weights(zb, xb) * wide).astype(jnp.bfloat16)
        inner = jnp.sum(pair(expert_out, zb, xb).astype(jnp.float32) * wide, axis=1, keepdims=True)
        for core in range(2):
            line = row_of(inner[core * tokens : (core + 1) * tokens])
            inner_out[first + core] = jnp.broadcast_to(line, inner_out.shape[1:])

            @pl.when(first + core != me)
            def _():
                start_one(*inner_way, first + core)

        hidden_grad = product(out_grad, down_ref[0], 1, 1)
        gate_grad = (hidden_grad * gate_factor[at]).astype(jnp.bfloat16)
        up_grad = (hidden_grad * up_factor[at]).astype(jnp.bfloat16)
        block = pair(rows, zb, xb)
        sums[0] += product(gate_grad, block, 0, 0)
        sums[1] += product(up_grad, block, 0, 0)
        sums[2] += product(hidden_all[at], out_grad, 0, 0)

    gather_blocks(senders, rows, row_send, row_recv, forward)
    by_distance(send_across)
    by_distance(send_along)
    mixture = out_total[...]
    mixture_ref[...] = mixture.astype(jnp.bfloat16)
    residual[me] = (mixture - judge_ref[...].astype(jnp.float32)).astype(jnp.bfloat16)
    sums[...] = jnp.zeros_like(sums)
    gather_blocks(senders, residual, residual_send, residual_recv, backward)
    inner_ref[me] = inner_out[me]
    grad_gate_ref[0] = sums[0].astype(jnp.bfloat16)
    grad_up_ref[0] = sums[1].astype(jnp.bfloat16)
    grad_down_ref[0] = sums[2].astype(jnp.bfloat16)
    by_distance(finish)
    to_each(*weight_way, sent_one)
    to_each(*inner_way, land_one)
    to_each(*inner_way, sent_one)


def vmem_specs(count):
    return [pl.BlockSpec(memory_space=pltpu.VMEM)] * count


def whole_layer(rows, weights, judge, w_gate, w_up, w_down):
    senders = weights.shape[0]
    depth = senders // 4
    pairs = senders // 2
    block = rows.shape
    tokens = block[0]
    units = w_gate.shape[1]
    dma = pltpu.SemaphoreType.DMA

    def blocks(count):
        return pltpu.VMEM((count, *block), jnp.bfloat16)

    def unit_blocks(dtype):
        return pltpu.VMEM((pairs, 2 * tokens, units), dtype)

    grad = jax.ShapeDtypeStruct(w_gate.shape, jnp.bfloat16)
    return pl.pallas_call(
        functools.partial(layer_kernel, senders),
        out_shape=(
            jax.ShapeDtypeStruct(block, jnp.bfloat16),
            jax.ShapeDtypeStruct(weights.shape, weights.dtype),
            grad,
            grad,
            grad,
        ),
        in_specs=vmem_specs(6),
        out_specs=tuple(vmem_specs(5)),
        scratch_shapes=[
            blocks(senders),
            pltpu.VMEM(weights.shape, weights.dtype),
            blocks(senders),
            blocks(senders),
            unit_blocks(jnp.bfloat16),
            unit_blocks(jnp.float32),
            unit_blocks(jnp.float32),
            blocks(senders),
            pltpu.VMEM(weights.shape, weights.dtype),
            pltpu.VMEM((3, *w_gate.shape[1:]), jnp.float32),
            blocks(2 * depth),
            blocks(depth),
            blocks(depth),
            blocks(depth),
            blocks(depth),
            blocks(depth),
            pltpu.VMEM(block, jnp.float32),
            dma((2 * depth,)),
            dma((2 * depth,)),
            dma((depth,)),
            dma((depth,)),
            dma((depth,)),
            dma((depth,)),
            dma((depth,)),
            dma((senders, 4)),
            dma((senders,)),
            dma((senders, 4)),
            dma((senders,)),
            dma((senders,)),
            dma((senders,)),
            dma((senders,)),
            dma((senders,)),
        ],
        compiler_params=pltpu.CompilerParams(
            collective_id=0, has_side_effects=True, vmem_limit_bytes=56 << 20
        ),
    )(rows, weights, judge, w_gate, w_up, w_down)


def dense_rows(student_input, judge_output, expert_ids, route_weights, w_gate, w_up, w_down):
    experts = lax.axis_size("expert")
    tok_count = student_input.shape[0]
    chosen = expert_ids[:, :, None] == jnp.arange(experts, dtype=jnp.int32)[None, None, :]
    dense_weights = jnp.sum(jnp.where(chosen, route_weights[:, :, None], 0.0), axis=1)
    lines = jnp.broadcast_to(dense_weights.T[:, None, :], (experts, 8, tok_count))
    mixture, inner, *grads = whole_layer(student_input, lines, judge_output, w_gate, w_up, w_down)
    route_grads = jnp.sum(jnp.where(chosen, inner[:, 0].T[:, None, :], 0.0), axis=2)
    return (mixture, route_grads, *grads)


def on_device(student_input, judge_output, expert_ids, route_weights, w_gate, w_up, w_down):
    experts = w_gate.shape[0] * lax.axis_size("expert")
    senders = lax.axis_size("expert")
    alone = w_gate.shape[0] == 1 and lax.axis_size("dp") == 1 and senders % 4 == 0
    dense = alone and experts <= 4 * expert_ids.shape[1]
    form = dense_rows if dense else routed_rows
    return form(student_input, judge_output, expert_ids, route_weights, w_gate, w_up, w_down)


def solution(mesh):
    placed = (
        P(("groups", "dp", "expert"), None),
        P(("groups", "dp", "expert"), None),
        P(("groups", "dp", "expert"), None),
        P(("groups", "dp", "expert"), None),
        P("expert", "dp", None),
        P("expert", "dp", None),
        P("expert", "dp", None),
    )
    return jax.shard_map(
        on_device,
        mesh=mesh,
        in_specs=placed,
        out_specs=(
            P(("groups", "dp", "expert"), None),
            P(("groups", "dp", "expert"), None),
            P(("groups", "expert"), "dp", None),
            P(("groups", "expert"), "dp", None),
            P(("groups", "expert"), "dp", None),
        ),
        check_vma=False,
    )
```

```python
import functools
import math

import jax
import jax.numpy as jnp
from jax import lax
from jax.experimental import pallas as pl
from jax.experimental.pallas import tpu as pltpu
from jax.sharding import PartitionSpec as P


def slot_layout(flat_ids, experts, capacity):
    pick_total = flat_ids.shape[0]
    span = math.gcd(pick_total, 128)
    count_blocks = pick_total // span
    onehot = (flat_ids[:, None] == jnp.arange(experts, dtype=jnp.int32)[None, :]).astype(
        jnp.bfloat16
    )
    onehot = onehot.reshape(count_blocks, span, experts)
    rows_here = jnp.arange(span, dtype=jnp.int32)
    lower = (rows_here[:, None] > rows_here[None, :]).astype(jnp.bfloat16)
    within = jnp.einsum("ij,bje->bie", lower, onehot, preferred_element_type=jnp.float32)
    totals = jnp.sum(onehot.astype(jnp.float32), axis=1)
    before = jnp.cumsum(totals, axis=0) - totals
    earlier = within + before[:, None, :]
    slot_index = jnp.sum(earlier * onehot.astype(jnp.float32), axis=2).reshape(-1).astype(jnp.int32)
    position = flat_ids * capacity + slot_index
    source = (
        jnp.zeros((experts * capacity,), jnp.int32)
        .at[position]
        .set(jnp.arange(1, pick_total + 1, dtype=jnp.int32))
    )
    return (position, source)


def hidden_units(row_block, gate_full, up_full):
    gate_pre = jnp.einsum("esd,efd->esf", row_block, gate_full, preferred_element_type=jnp.float32)
    up_pre = jnp.einsum("esd,efd->esf", row_block, up_full, preferred_element_type=jnp.float32)
    hidden = (gate_pre * jax.nn.sigmoid(gate_pre) * up_pre).astype(jnp.bfloat16)
    return (gate_pre, up_pre, hidden)


def routed_rows(student_input, judge_output, expert_ids, route_weights, w_gate, w_up, w_down):
    tok_count, dim_model = student_input.shape
    top_picks = expert_ids.shape[1]
    exp_local = w_gate.shape[0]
    senders = lax.axis_size("expert")
    experts = exp_local * senders
    capacity = min(tok_count, tok_count * top_picks * 5 // (4 * experts))
    flat_ids = expert_ids.reshape(-1)
    position, source = slot_layout(flat_ids, experts, capacity)
    is_valid = (source > 0)[:, None]
    pick_index = jnp.maximum(source - 1, 0)
    empty_rows = jnp.zeros((), jnp.bfloat16)
    send_rows = jnp.where(is_valid, student_input[pick_index // top_picks], empty_rows).reshape(
        experts, capacity, dim_model
    )
    gate_full, up_full, down_full = (
        lax.all_gather(w_gate, "dp", axis=1, tiled=True),
        lax.all_gather(w_up, "dp", axis=1, tiled=True),
        lax.all_gather(w_down, "dp", axis=1, tiled=True),
    )
    row_block = lax.all_to_all(send_rows, "expert", split_axis=0, concat_axis=1, tiled=True)
    gate_pre, up_pre, hidden = hidden_units(row_block, gate_full, up_full)
    expert_out = jnp.einsum(
        "esf,efd->esd", hidden, down_full, preferred_element_type=jnp.float32
    ).astype(jnp.bfloat16)
    returned = lax.all_to_all(
        expert_out, "expert", split_axis=1, concat_axis=0, tiled=True
    ).reshape(experts * capacity, dim_model)
    pick_out = returned[position].reshape(tok_count, top_picks, dim_model)
    pick_wide = pick_out.astype(jnp.float32)
    mixture = jnp.sum(route_weights[:, :, None] * pick_wide, axis=1)
    residual = mixture - judge_output.astype(jnp.float32)
    route_grads = jnp.sum(pick_wide * residual[:, None, :], axis=2)
    out_grad = (
        (route_weights[:, :, None] * residual[:, None, :])
        .astype(jnp.bfloat16)
        .reshape(tok_count * top_picks, dim_model)
    )
    send_grads = jnp.where(is_valid, out_grad[pick_index], empty_rows).reshape(
        experts, capacity, dim_model
    )
    grad_block = lax.all_to_all(send_grads, "expert", split_axis=0, concat_axis=1, tiled=True)
    hidden_grad = jnp.einsum(
        "esd,efd->esf", grad_block, down_full, preferred_element_type=jnp.float32
    )
    sig_gate = jax.nn.sigmoid(gate_pre)
    gate_grad = (hidden_grad * up_pre * sig_gate * (1.0 + gate_pre * (1.0 - sig_gate))).astype(
        jnp.bfloat16
    )
    up_grad = (hidden_grad * gate_pre * sig_gate).astype(jnp.bfloat16)
    gate_part = jnp.einsum("esf,esd->efd", gate_grad, row_block, preferred_element_type=jnp.float32)
    up_part = jnp.einsum("esf,esd->efd", up_grad, row_block, preferred_element_type=jnp.float32)
    down_part = jnp.einsum("esf,esd->efd", hidden, grad_block, preferred_element_type=jnp.float32)
    grad_gate, grad_up, grad_down = (
        lax.psum_scatter(
            gate_part.astype(jnp.bfloat16), "dp", scatter_dimension=1, tiled=True
        ).astype(jnp.float32),
        lax.psum_scatter(
            up_part.astype(jnp.bfloat16), "dp", scatter_dimension=1, tiled=True
        ).astype(jnp.float32),
        lax.psum_scatter(
            down_part.astype(jnp.bfloat16), "dp", scatter_dimension=1, tiled=True
        ).astype(jnp.float32),
    )
    return (
        mixture.astype(jnp.bfloat16),
        route_grads,
        grad_gate.astype(jnp.bfloat16),
        grad_up.astype(jnp.bfloat16),
        grad_down.astype(jnp.bfloat16),
    )


UP, DOWN, ACROSS, SIBLING = range(4)
MESH = pl.DeviceIdType.MESH


def place(senders):
    me = lax.axis_index("expert")
    depth = senders // 4
    z, x, c = me // 4, (me // 2) % 2, me % 2
    return depth, z, x, c


def index_of(z, x, c):
    return z * 4 + x * 2 + c


def remote(src, dst, send_sem, recv_sem, device):
    return pltpu.make_async_remote_copy(
        src_ref=src,
        dst_ref=dst,
        send_sem=send_sem,
        recv_sem=recv_sem,
        device_id={"expert": device},
        device_id_type=MESH,
    )


def greet_all(senders):
    me = lax.axis_index("expert")
    barrier = pltpu.get_barrier_semaphore()
    for step in range(1, senders):
        other = lax.rem(me + step, senders)
        pl.semaphore_signal(barrier, inc=1, device_id={"expert": other}, device_id_type=MESH)
    pl.semaphore_wait(barrier, senders - 1)


def gather_blocks(senders, out, send_sem, recv_sem, visit):
    depth, z, x, c = place(senders)
    targets = {
        UP: lambda: index_of(z + 1, x, c),
        DOWN: lambda: index_of(z - 1, x, c),
        ACROSS: lambda: index_of(z, 1 - x, c),
        SIBLING: lambda: index_of(z, x, 1 - c),
    }

    def copy(slot, way):
        return remote(
            out.at[slot], out.at[slot], send_sem.at[slot, way], recv_sem.at[slot], targets[way]()
        )

    def arrived(slot):
        copy(slot, ACROSS).wait_recv()

    def send_on(zb, act):
        slot = index_of(zb, x, c)
        pl.when((zb <= z) & (z < depth - 1))(lambda: act(copy(slot, UP)))
        pl.when((zb >= z) & (z > 0))(lambda: act(copy(slot, DOWN)))
        act(copy(slot, ACROSS))
        act(copy(slot, SIBLING))

    near = jnp.minimum(z, depth - 1 - z)

    def layer(p):
        both_sides = z + (p + 1) // 2 * (1 - 2 * (p % 2))
        one_side = jnp.where(z < depth - 1 - z, p, depth - 1 - p)
        return jnp.where(p <= 2 * near, both_sides, one_side)

    def column_arrival(p):
        zb = layer(p)
        arrived(index_of(zb, x, c))
        send_on(zb, lambda one: one.start())

    send_on(z, lambda one: one.start())

    @pl.loop(0, 2 * depth)
    def _(step):
        p = step // 2
        turn = step % 2
        zb = layer(p)

        @pl.when(turn == 1)
        def _():
            pl.when(p == 0)(lambda: column_arrival(1))
            pl.when(p + 2 < depth)(lambda: column_arrival(p + 2))
            slot = index_of(zb, 1 - x, c)
            arrived(slot)
            copy(slot, SIBLING).start()

        xb = x + turn * (1 - 2 * x)
        arrived(index_of(zb, xb, 1 - c))
        visit(zb, xb)

    @pl.loop(0, depth)
    def _(zb):
        send_on(zb, lambda one: one.wait_send())
        copy(index_of(zb, 1 - x, c), SIBLING).wait_send()


def column_of(row):
    size = row.shape[1]
    square = (size, size)
    diagonal = lax.broadcasted_iota(jnp.int32, square, 0) == lax.broadcasted_iota(
        jnp.int32, square, 1
    )
    return jnp.sum(jnp.where(diagonal, row, 0.0), axis=1, keepdims=True)


def row_of(column):
    size = column.shape[0]
    square = (size, size)
    diagonal = lax.broadcasted_iota(jnp.int32, square, 0) == lax.broadcasted_iota(
        jnp.int32, square, 1
    )
    return jnp.sum(jnp.where(diagonal, column, 0.0), axis=0, keepdims=True)


def product(left, right, left_dim, right_dim):
    return lax.dot_general(
        left, right, (((left_dim,), (right_dim,)), ((), ())), preferred_element_type=jnp.float32
    )


def layer_kernel(
    senders,
    row_ref,
    weight_ref,
    judge_ref,
    gate_ref,
    up_ref,
    down_ref,
    mixture_ref,
    inner_ref,
    grad_gate_ref,
    grad_up_ref,
    grad_down_ref,
    rows,
    weights,
    part_ref,
    expert_out,
    hidden_all,
    gate_factor,
    up_factor,
    residual,
    inner_out,
    sums,
    sib_in,
    x_out,
    x_in,
    z_out,
    up_in,
    down_in,
    out_total,
    sib_send,
    sib_recv,
    x_send,
    x_recv,
    z_send,
    up_recv,
    down_recv,
    row_send,
    row_recv,
    residual_send,
    residual_recv,
    weight_send,
    weight_recv,
    inner_send,
    inner_recv,
):
    me = lax.axis_index("expert")
    depth, z, x, c = place(senders)
    tokens, dim_model = row_ref.shape
    rows[me] = row_ref[...]
    weights[me] = weight_ref[me]
    greet_all(senders)

    def to_each(src, dst, send, recv, act):
        @pl.loop(1, senders)
        def _(step):
            other = lax.rem(me + step, senders)
            act(src, dst, send, recv, other)

    def start_one(src, dst, send, recv, other):
        remote(src.at[other], dst.at[me], send.at[other], recv.at[me], other).start()

    def land_one(src, dst, send, recv, other):
        remote(src.at[other], dst.at[other], send.at[other], recv.at[other], other).wait_recv()

    def sent_one(src, dst, send, recv, other):
        remote(src.at[other], dst.at[me], send.at[other], recv.at[me], other).wait_send()

    weight_way = (weight_ref, weights, weight_send, weight_recv)
    inner_way = (inner_out, inner_ref, inner_send, inner_recv)
    to_each(*weight_way, start_one)

    def by_distance(act):
        for d in range(depth - 1, 0, -1):
            pl.when(z + d < depth)(functools.partial(act, z + d, UP))
            pl.when(z - d >= 0)(functools.partial(act, z - d, DOWN))
        act(z, None)

    def sib_copy(zb, xb):
        slot = zb * 2 + xb
        return remote(
            part_ref.at[index_of(zb, xb, 1 - c)],
            sib_in.at[slot],
            sib_send.at[slot],
            sib_recv.at[slot],
            index_of(z, x, 1 - c),
        )

    def x_copy(zb):
        return remote(
            x_out.at[zb], x_in.at[zb], x_send.at[zb], x_recv.at[zb], index_of(z, 1 - x, c)
        )

    def up_copy(zb):
        return remote(
            z_out.at[zb], up_in.at[zb], z_send.at[zb], up_recv.at[zb], index_of(z + 1, x, c)
        )

    def down_copy(zb):
        return remote(
            z_out.at[zb], down_in.at[zb], z_send.at[zb], down_recv.at[zb], index_of(z - 1, x, c)
        )

    def pair(ref, zb, xb):
        first = index_of(zb, xb, 0)
        return jnp.concatenate([ref[first], ref[first + 1]], axis=0)

    def pair_weights(zb, xb):
        first = index_of(zb, xb, 0)
        return jnp.concatenate(
            [column_of(weights[first][:1]), column_of(weights[first + 1][:1])], axis=0
        )

    def forward(zb, xb):
        first, at = index_of(zb, xb, 0), zb * 2 + xb
        for core in range(2):

            @pl.when(first + core != me)
            def _():
                land_one(*weight_way, first + core)

        block = pair(rows, zb, xb)
        gate_pre = product(block, gate_ref[0], 1, 1)
        up_pre = product(block, up_ref[0], 1, 1)
        sig_gate = jax.nn.sigmoid(gate_pre)
        silu = gate_pre * sig_gate
        hidden = (silu * up_pre).astype(jnp.bfloat16)
        hidden_all[at] = hidden
        up_factor[at] = silu
        gate_factor[at] = up_pre * sig_gate * (1.0 + gate_pre * (1.0 - sig_gate))
        made = product(hidden, down_ref[0], 1, 0).astype(jnp.bfloat16)
        weighted = (pair_weights(zb, xb) * made.astype(jnp.float32)).astype(jnp.bfloat16)
        for core in range(2):
            expert_out[first + core] = made[core * tokens : (core + 1) * tokens]
            part_ref[first + core] = weighted[core * tokens : (core + 1) * tokens]
        sib_copy(zb, xb).start()

    def pair_sum(zb, xb):
        mine = part_ref[index_of(zb, xb, c)].astype(jnp.float32)
        return mine + sib_in[zb * 2 + xb].astype(jnp.float32)

    def send_across(zb, way):
        sib_copy(zb, 1 - x).wait_recv()
        x_out[zb] = pair_sum(zb, 1 - x).astype(jnp.bfloat16)
        x_copy(zb).start()

    def send_along(zb, way):
        sib_copy(zb, x).wait_recv()
        x_copy(zb).wait_recv()
        out_total[...] = pair_sum(zb, x) + x_in[zb].astype(jnp.float32)
        if way != DOWN:

            @pl.when(z > 0)
            def _():
                up_copy(zb).wait_recv()
                out_total[...] += up_in[zb].astype(jnp.float32)

        if way != UP:

            @pl.when(z < depth - 1)
            def _():
                down_copy(zb).wait_recv()
                out_total[...] += down_in[zb].astype(jnp.float32)

        if way is not None:
            z_out[zb] = out_total[...].astype(jnp.bfloat16)
            (up_copy if way == UP else down_copy)(zb).start()

    def finish(zb, way):
        sib_copy(zb, 1 - x).wait_send()
        sib_copy(zb, x).wait_send()
        x_copy(zb).wait_send()
        if way is not None:
            (up_copy if way == UP else down_copy)(zb).wait_send()

    def backward(zb, xb):
        first, at = index_of(zb, xb, 0), zb * 2 + xb
        wide = pair(residual, zb, xb).astype(jnp.float32)
        out_grad = (pair_weights(zb, xb) * wide).astype(jnp.bfloat16)
        inner = jnp.sum(pair(expert_out, zb, xb).astype(jnp.float32) * wide, axis=1, keepdims=True)
        for core in range(2):
            line = row_of(inner[core * tokens : (core + 1) * tokens])
            inner_out[first + core] = jnp.broadcast_to(line, inner_out.shape[1:])

            @pl.when(first + core != me)
            def _():
                start_one(*inner_way, first + core)

        hidden_grad = product(out_grad, down_ref[0], 1, 1)
        gate_grad = (hidden_grad * gate_factor[at]).astype(jnp.bfloat16)
        up_grad = (hidden_grad * up_factor[at]).astype(jnp.bfloat16)
        block = pair(rows, zb, xb)
        sums[0] += product(gate_grad, block, 0, 0)
        sums[1] += product(up_grad, block, 0, 0)
        sums[2] += product(hidden_all[at], out_grad, 0, 0)

    gather_blocks(senders, rows, row_send, row_recv, forward)
    by_distance(send_across)
    by_distance(send_along)
    mixture = out_total[...]
    mixture_ref[...] = mixture.astype(jnp.bfloat16)
    residual[me] = (mixture - judge_ref[...].astype(jnp.float32)).astype(jnp.bfloat16)
    sums[...] = jnp.zeros_like(sums)
    gather_blocks(senders, residual, residual_send, residual_recv, backward)
    inner_ref[me] = inner_out[me]
    grad_gate_ref[0] = sums[0].astype(jnp.bfloat16)
    grad_up_ref[0] = sums[1].astype(jnp.bfloat16)
    grad_down_ref[0] = sums[2].astype(jnp.bfloat16)
    by_distance(finish)
    to_each(*weight_way, sent_one)
    to_each(*inner_way, land_one)
    to_each(*inner_way, sent_one)


def vmem_specs(count):
    return [pl.BlockSpec(memory_space=pltpu.VMEM)] * count


def whole_layer(rows, weights, judge, w_gate, w_up, w_down):
    senders = weights.shape[0]
    depth = senders // 4
    pairs = senders // 2
    block = rows.shape
    tokens = block[0]
    units = w_gate.shape[1]
    dma = pltpu.SemaphoreType.DMA

    def blocks(count):
        return pltpu.VMEM((count, *block), jnp.bfloat16)

    def unit_blocks(dtype):
        return pltpu.VMEM((pairs, 2 * tokens, units), dtype)

    grad = jax.ShapeDtypeStruct(w_gate.shape, jnp.bfloat16)
    return pl.pallas_call(
        functools.partial(layer_kernel, senders),
        out_shape=(
            jax.ShapeDtypeStruct(block, jnp.bfloat16),
            jax.ShapeDtypeStruct(weights.shape, weights.dtype),
            grad,
            grad,
            grad,
        ),
        in_specs=vmem_specs(6),
        out_specs=tuple(vmem_specs(5)),
        scratch_shapes=[
            blocks(senders),
            pltpu.VMEM(weights.shape, weights.dtype),
            blocks(senders),
            blocks(senders),
            unit_blocks(jnp.bfloat16),
            unit_blocks(jnp.float32),
            unit_blocks(jnp.float32),
            blocks(senders),
            pltpu.VMEM(weights.shape, weights.dtype),
            pltpu.VMEM((3, *w_gate.shape[1:]), jnp.float32),
            blocks(2 * depth),
            blocks(depth),
            blocks(depth),
            blocks(depth),
            blocks(depth),
            blocks(depth),
            pltpu.VMEM(block, jnp.float32),
            dma((2 * depth,)),
            dma((2 * depth,)),
            dma((depth,)),
            dma((depth,)),
            dma((depth,)),
            dma((depth,)),
            dma((depth,)),
            dma((senders, 4)),
            dma((senders,)),
            dma((senders, 4)),
            dma((senders,)),
            dma((senders,)),
            dma((senders,)),
            dma((senders,)),
            dma((senders,)),
        ],
        compiler_params=pltpu.CompilerParams(
            collective_id=0, has_side_effects=True, vmem_limit_bytes=56 << 20
        ),
    )(rows, weights, judge, w_gate, w_up, w_down)


def dense_rows(student_input, judge_output, expert_ids, route_weights, w_gate, w_up, w_down):
    experts = lax.axis_size("expert")
    tok_count = student_input.shape[0]
    chosen = expert_ids[:, :, None] == jnp.arange(experts, dtype=jnp.int32)[None, None, :]
    dense_weights = jnp.sum(jnp.where(chosen, route_weights[:, :, None], 0.0), axis=1)
    lines = jnp.broadcast_to(dense_weights.T[:, None, :], (experts, 8, tok_count))
    mixture, inner, *grads = whole_layer(student_input, lines, judge_output, w_gate, w_up, w_down)
    route_grads = jnp.sum(jnp.where(chosen, inner[:, 0].T[:, None, :], 0.0), axis=2)
    return (mixture, route_grads, *grads)


def on_device(student_input, judge_output, expert_ids, route_weights, w_gate, w_up, w_down):
    experts = w_gate.shape[0] * lax.axis_size("expert")
    senders = lax.axis_size("expert")
    alone = w_gate.shape[0] == 1 and lax.axis_size("dp") == 1 and senders % 4 == 0 and senders > 4
    dense = alone and experts <= 4 * expert_ids.shape[1]
    form = dense_rows if dense else routed_rows
    return form(student_input, judge_output, expert_ids, route_weights, w_gate, w_up, w_down)


def solution(mesh):
    placed = (
        P(("groups", "dp", "expert"), None),
        P(("groups", "dp", "expert"), None),
        P(("groups", "dp", "expert"), None),
        P(("groups", "dp", "expert"), None),
        P("expert", "dp", None),
        P("expert", "dp", None),
        P("expert", "dp", None),
    )
    return jax.shard_map(
        on_device,
        mesh=mesh,
        in_specs=placed,
        out_specs=(
            P(("groups", "dp", "expert"), None),
            P(("groups", "dp", "expert"), None),
            P(("groups", "expert"), "dp", None),
            P(("groups", "expert"), "dp", None),
            P(("groups", "expert"), "dp", None),
        ),
        check_vma=False,
    )
```

```python
import functools
import math

import jax
import jax.numpy as jnp
from jax import lax
from jax.experimental import pallas as pl
from jax.experimental.pallas import tpu as pltpu
from jax.sharding import PartitionSpec as P


def slot_layout(flat_ids, experts, capacity):
    pick_total = flat_ids.shape[0]
    span = math.gcd(pick_total, 128)
    count_blocks = pick_total // span
    onehot = (flat_ids[:, None] == jnp.arange(experts, dtype=jnp.int32)[None, :]).astype(
        jnp.bfloat16
    )
    onehot = onehot.reshape(count_blocks, span, experts)
    rows_here = jnp.arange(span, dtype=jnp.int32)
    lower = (rows_here[:, None] > rows_here[None, :]).astype(jnp.bfloat16)
    within = jnp.einsum("ij,bje->bie", lower, onehot, preferred_element_type=jnp.float32)
    totals = jnp.sum(onehot.astype(jnp.float32), axis=1)
    before = jnp.cumsum(totals, axis=0) - totals
    earlier = within + before[:, None, :]
    slot_index = jnp.sum(earlier * onehot.astype(jnp.float32), axis=2).reshape(-1).astype(jnp.int32)
    position = flat_ids * capacity + slot_index
    source = (
        jnp.zeros((experts * capacity,), jnp.int32)
        .at[position]
        .set(jnp.arange(1, pick_total + 1, dtype=jnp.int32))
    )
    return (position, source)


def hidden_units(row_block, gate_full, up_full):
    gate_pre = jnp.einsum("esd,efd->esf", row_block, gate_full, preferred_element_type=jnp.float32)
    up_pre = jnp.einsum("esd,efd->esf", row_block, up_full, preferred_element_type=jnp.float32)
    hidden = (gate_pre * jax.nn.sigmoid(gate_pre) * up_pre).astype(jnp.bfloat16)
    return (gate_pre, up_pre, hidden)


def routed_rows(student_input, judge_output, expert_ids, route_weights, w_gate, w_up, w_down):
    tok_count, dim_model = student_input.shape
    top_picks = expert_ids.shape[1]
    exp_local = w_gate.shape[0]
    senders = lax.axis_size("expert")
    experts = exp_local * senders
    capacity = min(tok_count, tok_count * top_picks * 5 // (4 * experts))
    flat_ids = expert_ids.reshape(-1)
    position, source = slot_layout(flat_ids, experts, capacity)
    is_valid = (source > 0)[:, None]
    pick_index = jnp.maximum(source - 1, 0)
    empty_rows = jnp.zeros((), jnp.bfloat16)
    send_rows = jnp.where(is_valid, student_input[pick_index // top_picks], empty_rows).reshape(
        experts, capacity, dim_model
    )
    gate_full, up_full, down_full = (
        lax.all_gather(w_gate, "dp", axis=1, tiled=True),
        lax.all_gather(w_up, "dp", axis=1, tiled=True),
        lax.all_gather(w_down, "dp", axis=1, tiled=True),
    )
    row_block = lax.all_to_all(send_rows, "expert", split_axis=0, concat_axis=1, tiled=True)
    gate_pre, up_pre, hidden = hidden_units(row_block, gate_full, up_full)
    expert_out = jnp.einsum(
        "esf,efd->esd", hidden, down_full, preferred_element_type=jnp.float32
    ).astype(jnp.bfloat16)
    returned = lax.all_to_all(
        expert_out, "expert", split_axis=1, concat_axis=0, tiled=True
    ).reshape(experts * capacity, dim_model)
    pick_out = returned[position].reshape(tok_count, top_picks, dim_model)
    pick_wide = pick_out.astype(jnp.float32)
    mixture = jnp.sum(route_weights[:, :, None] * pick_wide, axis=1)
    residual = mixture - judge_output.astype(jnp.float32)
    route_grads = jnp.sum(pick_wide * residual[:, None, :], axis=2)
    out_grad = (
        (route_weights[:, :, None] * residual[:, None, :])
        .astype(jnp.bfloat16)
        .reshape(tok_count * top_picks, dim_model)
    )
    send_grads = jnp.where(is_valid, out_grad[pick_index], empty_rows).reshape(
        experts, capacity, dim_model
    )
    grad_block = lax.all_to_all(send_grads, "expert", split_axis=0, concat_axis=1, tiled=True)
    hidden_grad = jnp.einsum(
        "esd,efd->esf", grad_block, down_full, preferred_element_type=jnp.float32
    )
    sig_gate = jax.nn.sigmoid(gate_pre)
    gate_grad = (hidden_grad * up_pre * sig_gate * (1.0 + gate_pre * (1.0 - sig_gate))).astype(
        jnp.bfloat16
    )
    up_grad = (hidden_grad * gate_pre * sig_gate).astype(jnp.bfloat16)
    gate_part = jnp.einsum("esf,esd->efd", gate_grad, row_block, preferred_element_type=jnp.float32)
    up_part = jnp.einsum("esf,esd->efd", up_grad, row_block, preferred_element_type=jnp.float32)
    down_part = jnp.einsum("esf,esd->efd", hidden, grad_block, preferred_element_type=jnp.float32)
    grad_gate, grad_up, grad_down = (
        lax.psum_scatter(
            gate_part.astype(jnp.bfloat16), "dp", scatter_dimension=1, tiled=True
        ).astype(jnp.float32),
        lax.psum_scatter(
            up_part.astype(jnp.bfloat16), "dp", scatter_dimension=1, tiled=True
        ).astype(jnp.float32),
        lax.psum_scatter(
            down_part.astype(jnp.bfloat16), "dp", scatter_dimension=1, tiled=True
        ).astype(jnp.float32),
    )
    return (
        mixture.astype(jnp.bfloat16),
        route_grads,
        grad_gate.astype(jnp.bfloat16),
        grad_up.astype(jnp.bfloat16),
        grad_down.astype(jnp.bfloat16),
    )


UP, DOWN, ACROSS, SIBLING = range(4)
MESH = pl.DeviceIdType.MESH


def place(senders):
    me = lax.axis_index("expert")
    depth = senders // 4
    z, x, c = me // 4, (me // 2) % 2, me % 2
    return depth, z, x, c


def index_of(z, x, c):
    return z * 4 + x * 2 + c


def remote(src, dst, send_sem, recv_sem, device):
    return pltpu.make_async_remote_copy(
        src_ref=src,
        dst_ref=dst,
        send_sem=send_sem,
        recv_sem=recv_sem,
        device_id={"expert": device},
        device_id_type=MESH,
    )


def greet_all(senders):
    me = lax.axis_index("expert")
    barrier = pltpu.get_barrier_semaphore()
    for step in range(1, senders):
        other = lax.rem(me + step, senders)
        pl.semaphore_signal(barrier, inc=1, device_id={"expert": other}, device_id_type=MESH)
    pl.semaphore_wait(barrier, senders - 1)


def gather_blocks(senders, out, send_sem, recv_sem, visit):
    depth, z, x, c = place(senders)
    targets = {
        UP: lambda: index_of(z + 1, x, c),
        DOWN: lambda: index_of(z - 1, x, c),
        ACROSS: lambda: index_of(z, 1 - x, c),
        SIBLING: lambda: index_of(z, x, 1 - c),
    }

    def copy(slot, way):
        return remote(
            out.at[slot], out.at[slot], send_sem.at[slot, way], recv_sem.at[slot], targets[way]()
        )

    def arrived(slot):
        copy(slot, ACROSS).wait_recv()

    def send_on(zb, act):
        slot = index_of(zb, x, c)
        pl.when((zb <= z) & (z < depth - 1))(lambda: act(copy(slot, UP)))
        pl.when((zb >= z) & (z > 0))(lambda: act(copy(slot, DOWN)))
        act(copy(slot, ACROSS))
        act(copy(slot, SIBLING))

    near = jnp.minimum(z, depth - 1 - z)

    def layer(p):
        both_sides = z + (p + 1) // 2 * (1 - 2 * (p % 2))
        one_side = jnp.where(z < depth - 1 - z, p, depth - 1 - p)
        return jnp.where(p <= 2 * near, both_sides, one_side)

    def column_arrival(p):
        zb = layer(p)
        arrived(index_of(zb, x, c))
        send_on(zb, lambda one: one.start())

    send_on(z, lambda one: one.start())

    @pl.loop(0, 2 * depth)
    def _(step):
        p = step // 2
        turn = step % 2
        zb = layer(p)

        @pl.when(turn == 1)
        def _():
            pl.when(p == 0)(lambda: column_arrival(1))
            pl.when(p + 2 < depth)(lambda: column_arrival(p + 2))
            slot = index_of(zb, 1 - x, c)
            arrived(slot)
            copy(slot, SIBLING).start()

        xb = x + turn * (1 - 2 * x)
        arrived(index_of(zb, xb, 1 - c))
        visit(zb, xb)

    @pl.loop(0, depth)
    def _(zb):
        send_on(zb, lambda one: one.wait_send())
        copy(index_of(zb, 1 - x, c), SIBLING).wait_send()


def column_of(row):
    size = row.shape[1]
    square = (size, size)
    diagonal = lax.broadcasted_iota(jnp.int32, square, 0) == lax.broadcasted_iota(
        jnp.int32, square, 1
    )
    return jnp.sum(jnp.where(diagonal, row, 0.0), axis=1, keepdims=True)


def row_of(column):
    size = column.shape[0]
    square = (size, size)
    diagonal = lax.broadcasted_iota(jnp.int32, square, 0) == lax.broadcasted_iota(
        jnp.int32, square, 1
    )
    return jnp.sum(jnp.where(diagonal, column, 0.0), axis=0, keepdims=True)


def product(left, right, left_dim, right_dim):
    return lax.dot_general(
        left, right, (((left_dim,), (right_dim,)), ((), ())), preferred_element_type=jnp.float32
    )


def layer_kernel(
    senders,
    row_ref,
    weight_ref,
    judge_ref,
    gate_ref,
    up_ref,
    down_ref,
    mixture_ref,
    inner_ref,
    grad_gate_ref,
    grad_up_ref,
    grad_down_ref,
    rows,
    weights,
    part_ref,
    expert_out,
    hidden_all,
    gate_factor,
    up_factor,
    residual,
    inner_out,
    sums,
    sib_in,
    x_out,
    x_in,
    z_out,
    up_in,
    down_in,
    out_total,
    sib_send,
    sib_recv,
    x_send,
    x_recv,
    z_send,
    up_recv,
    down_recv,
    row_send,
    row_recv,
    residual_send,
    residual_recv,
    weight_send,
    weight_recv,
    inner_send,
    inner_recv,
):
    me = lax.axis_index("expert")
    depth, z, x, c = place(senders)
    tokens, dim_model = row_ref.shape
    rows[me] = row_ref[...]
    weights[me] = weight_ref[me]
    greet_all(senders)

    def to_each(src, dst, send, recv, act):
        @pl.loop(1, senders)
        def _(step):
            other = lax.rem(me + step, senders)
            act(src, dst, send, recv, other)

    def start_one(src, dst, send, recv, other):
        remote(src.at[other], dst.at[me], send.at[other], recv.at[me], other).start()

    def land_one(src, dst, send, recv, other):
        remote(src.at[other], dst.at[other], send.at[other], recv.at[other], other).wait_recv()

    def sent_one(src, dst, send, recv, other):
        remote(src.at[other], dst.at[me], send.at[other], recv.at[me], other).wait_send()

    weight_way = (weight_ref, weights, weight_send, weight_recv)
    inner_way = (inner_out, inner_ref, inner_send, inner_recv)
    to_each(*weight_way, start_one)

    def by_distance(act):
        for d in range(depth - 1, 0, -1):
            pl.when(z + d < depth)(functools.partial(act, z + d, UP))
            pl.when(z - d >= 0)(functools.partial(act, z - d, DOWN))
        act(z, None)

    def sib_copy(zb, xb):
        slot = zb * 2 + xb
        return remote(
            part_ref.at[index_of(zb, xb, 1 - c)],
            sib_in.at[slot],
            sib_send.at[slot],
            sib_recv.at[slot],
            index_of(z, x, 1 - c),
        )

    def x_copy(zb):
        return remote(
            x_out.at[zb], x_in.at[zb], x_send.at[zb], x_recv.at[zb], index_of(z, 1 - x, c)
        )

    def up_copy(zb):
        return remote(
            z_out.at[zb], up_in.at[zb], z_send.at[zb], up_recv.at[zb], index_of(z + 1, x, c)
        )

    def down_copy(zb):
        return remote(
            z_out.at[zb], down_in.at[zb], z_send.at[zb], down_recv.at[zb], index_of(z - 1, x, c)
        )

    def pair(ref, zb, xb):
        first = index_of(zb, xb, 0)
        return jnp.concatenate([ref[first], ref[first + 1]], axis=0)

    def pair_weights(zb, xb):
        first = index_of(zb, xb, 0)
        return jnp.concatenate(
            [column_of(weights[first][:1]), column_of(weights[first + 1][:1])], axis=0
        )

    def forward(zb, xb):
        first, at = index_of(zb, xb, 0), zb * 2 + xb
        for core in range(2):

            @pl.when(first + core != me)
            def _():
                land_one(*weight_way, first + core)

        block = pair(rows, zb, xb)
        gate_pre = product(block, gate_ref[0], 1, 1)
        up_pre = product(block, up_ref[0], 1, 1)
        sig_gate = jax.nn.sigmoid(gate_pre)
        silu = gate_pre * sig_gate
        hidden = (silu * up_pre).astype(jnp.bfloat16)
        hidden_all[at] = hidden
        up_factor[at] = silu
        gate_factor[at] = up_pre * sig_gate * (1.0 + gate_pre * (1.0 - sig_gate))
        made = product(hidden, down_ref[0], 1, 0).astype(jnp.bfloat16)
        weighted = (pair_weights(zb, xb) * made.astype(jnp.float32)).astype(jnp.bfloat16)
        for core in range(2):
            expert_out[first + core] = made[core * tokens : (core + 1) * tokens]
            part_ref[first + core] = weighted[core * tokens : (core + 1) * tokens]
        sib_copy(zb, xb).start()

    def pair_sum(zb, xb):
        mine = part_ref[index_of(zb, xb, c)].astype(jnp.float32)
        return mine + sib_in[zb * 2 + xb].astype(jnp.float32)

    def send_across(zb, way):
        sib_copy(zb, 1 - x).wait_recv()
        x_out[zb] = pair_sum(zb, 1 - x).astype(jnp.bfloat16)
        x_copy(zb).start()

    def send_along(zb, way):
        sib_copy(zb, x).wait_recv()
        x_copy(zb).wait_recv()
        out_total[...] = pair_sum(zb, x) + x_in[zb].astype(jnp.float32)
        if way != DOWN:

            @pl.when(z > 0)
            def _():
                up_copy(zb).wait_recv()
                out_total[...] += up_in[zb].astype(jnp.float32)

        if way != UP:

            @pl.when(z < depth - 1)
            def _():
                down_copy(zb).wait_recv()
                out_total[...] += down_in[zb].astype(jnp.float32)

        if way is not None:
            z_out[zb] = out_total[...].astype(jnp.bfloat16)
            (up_copy if way == UP else down_copy)(zb).start()

    def finish(zb, way):
        sib_copy(zb, 1 - x).wait_send()
        sib_copy(zb, x).wait_send()
        x_copy(zb).wait_send()
        if way is not None:
            (up_copy if way == UP else down_copy)(zb).wait_send()

    def backward(zb, xb):
        first, at = index_of(zb, xb, 0), zb * 2 + xb
        wide = pair(residual, zb, xb).astype(jnp.float32)
        out_grad = (pair_weights(zb, xb) * wide).astype(jnp.bfloat16)
        inner = jnp.sum(pair(expert_out, zb, xb).astype(jnp.float32) * wide, axis=1, keepdims=True)
        for core in range(2):
            line = row_of(inner[core * tokens : (core + 1) * tokens])
            inner_out[first + core] = jnp.broadcast_to(line, inner_out.shape[1:])

            @pl.when(first + core != me)
            def _():
                start_one(*inner_way, first + core)

        hidden_grad = product(out_grad, down_ref[0], 1, 1)
        gate_grad = (hidden_grad * gate_factor[at]).astype(jnp.bfloat16)
        up_grad = (hidden_grad * up_factor[at]).astype(jnp.bfloat16)
        block = pair(rows, zb, xb)
        sums[0] += product(gate_grad, block, 0, 0)
        sums[1] += product(up_grad, block, 0, 0)
        sums[2] += product(hidden_all[at], out_grad, 0, 0)

    gather_blocks(senders, rows, row_send, row_recv, forward)
    by_distance(send_across)
    sums[...] = jnp.zeros_like(sums)
    by_distance(send_along)
    mixture = out_total[...]
    mixture_ref[...] = mixture.astype(jnp.bfloat16)
    residual[me] = (mixture - judge_ref[...].astype(jnp.float32)).astype(jnp.bfloat16)
    gather_blocks(senders, residual, residual_send, residual_recv, backward)
    inner_ref[me] = inner_out[me]
    grad_gate_ref[0] = sums[0].astype(jnp.bfloat16)
    grad_up_ref[0] = sums[1].astype(jnp.bfloat16)
    grad_down_ref[0] = sums[2].astype(jnp.bfloat16)
    by_distance(finish)
    to_each(*weight_way, sent_one)
    to_each(*inner_way, land_one)
    to_each(*inner_way, sent_one)


def vmem_specs(count):
    return [pl.BlockSpec(memory_space=pltpu.VMEM)] * count


def whole_layer(rows, weights, judge, w_gate, w_up, w_down):
    senders = weights.shape[0]
    depth = senders // 4
    pairs = senders // 2
    block = rows.shape
    tokens = block[0]
    units = w_gate.shape[1]
    dma = pltpu.SemaphoreType.DMA

    def blocks(count):
        return pltpu.VMEM((count, *block), jnp.bfloat16)

    def unit_blocks(dtype):
        return pltpu.VMEM((pairs, 2 * tokens, units), dtype)

    grad = jax.ShapeDtypeStruct(w_gate.shape, jnp.bfloat16)
    return pl.pallas_call(
        functools.partial(layer_kernel, senders),
        out_shape=(
            jax.ShapeDtypeStruct(block, jnp.bfloat16),
            jax.ShapeDtypeStruct(weights.shape, weights.dtype),
            grad,
            grad,
            grad,
        ),
        in_specs=vmem_specs(6),
        out_specs=tuple(vmem_specs(5)),
        scratch_shapes=[
            blocks(senders),
            pltpu.VMEM(weights.shape, weights.dtype),
            blocks(senders),
            blocks(senders),
            unit_blocks(jnp.bfloat16),
            unit_blocks(jnp.float32),
            unit_blocks(jnp.float32),
            blocks(senders),
            pltpu.VMEM(weights.shape, weights.dtype),
            pltpu.VMEM((3, *w_gate.shape[1:]), jnp.float32),
            blocks(2 * depth),
            blocks(depth),
            blocks(depth),
            blocks(depth),
            blocks(depth),
            blocks(depth),
            pltpu.VMEM(block, jnp.float32),
            dma((2 * depth,)),
            dma((2 * depth,)),
            dma((depth,)),
            dma((depth,)),
            dma((depth,)),
            dma((depth,)),
            dma((depth,)),
            dma((senders, 4)),
            dma((senders,)),
            dma((senders, 4)),
            dma((senders,)),
            dma((senders,)),
            dma((senders,)),
            dma((senders,)),
            dma((senders,)),
        ],
        compiler_params=pltpu.CompilerParams(
            collective_id=0, has_side_effects=True, vmem_limit_bytes=56 << 20
        ),
    )(rows, weights, judge, w_gate, w_up, w_down)


def hand_on(*arrays):
    count = len(arrays)

    def kernel(*refs):
        for src, dst in zip(refs[:count], refs[count:]):
            dst[...] = src[...]

    return pl.pallas_call(
        kernel,
        out_shape=tuple(jax.ShapeDtypeStruct(a.shape, a.dtype) for a in arrays),
        in_specs=vmem_specs(count),
        out_specs=tuple(vmem_specs(count)),
        compiler_params=pltpu.CompilerParams(vmem_limit_bytes=16 << 20),
    )(*arrays)


def dense_rows(student_input, judge_output, expert_ids, route_weights, w_gate, w_up, w_down):
    experts = lax.axis_size("expert")
    tok_count = student_input.shape[0]
    chosen = expert_ids[:, :, None] == jnp.arange(experts, dtype=jnp.int32)[None, None, :]
    dense_weights = jnp.sum(jnp.where(chosen, route_weights[:, :, None], 0.0), axis=1)
    lines = jnp.broadcast_to(dense_weights.T[:, None, :], (experts, 8, tok_count))
    mixture, inner, *grads = whole_layer(student_input, lines, judge_output, w_gate, w_up, w_down)
    route_grads = jnp.sum(jnp.where(chosen, inner[:, 0].T[:, None, :], 0.0), axis=2)
    mixture, *grads = hand_on(mixture, *grads)
    return (mixture, route_grads, *grads)


def on_device(student_input, judge_output, expert_ids, route_weights, w_gate, w_up, w_down):
    experts = w_gate.shape[0] * lax.axis_size("expert")
    senders = lax.axis_size("expert")
    alone = w_gate.shape[0] == 1 and lax.axis_size("dp") == 1 and senders % 4 == 0 and senders > 4
    dense = alone and experts <= 4 * expert_ids.shape[1]
    form = dense_rows if dense else routed_rows
    return form(student_input, judge_output, expert_ids, route_weights, w_gate, w_up, w_down)


def solution(mesh):
    placed = (
        P(("groups", "dp", "expert"), None),
        P(("groups", "dp", "expert"), None),
        P(("groups", "dp", "expert"), None),
        P(("groups", "dp", "expert"), None),
        P("expert", "dp", None),
        P("expert", "dp", None),
        P("expert", "dp", None),
    )
    return jax.shard_map(
        on_device,
        mesh=mesh,
        in_specs=placed,
        out_specs=(
            P(("groups", "dp", "expert"), None),
            P(("groups", "dp", "expert"), None),
            P(("groups", "expert"), "dp", None),
            P(("groups", "expert"), "dp", None),
            P(("groups", "expert"), "dp", None),
        ),
        check_vma=False,
    )
```

```python
import functools
import math

import jax
import jax.numpy as jnp
from jax import lax
from jax.experimental import pallas as pl
from jax.experimental.pallas import tpu as pltpu
from jax.sharding import PartitionSpec as P


def slot_layout(flat_ids, experts, capacity):
    pick_total = flat_ids.shape[0]
    span = math.gcd(pick_total, 128)
    count_blocks = pick_total // span
    onehot = (flat_ids[:, None] == jnp.arange(experts, dtype=jnp.int32)[None, :]).astype(
        jnp.bfloat16
    )
    onehot = onehot.reshape(count_blocks, span, experts)
    rows_here = jnp.arange(span, dtype=jnp.int32)
    lower = (rows_here[:, None] > rows_here[None, :]).astype(jnp.bfloat16)
    within = jnp.einsum("ij,bje->bie", lower, onehot, preferred_element_type=jnp.float32)
    totals = jnp.sum(onehot.astype(jnp.float32), axis=1)
    before = jnp.cumsum(totals, axis=0) - totals
    earlier = within + before[:, None, :]
    slot_index = jnp.sum(earlier * onehot.astype(jnp.float32), axis=2).reshape(-1).astype(jnp.int32)
    position = flat_ids * capacity + slot_index
    source = (
        jnp.zeros((experts * capacity,), jnp.int32)
        .at[position]
        .set(jnp.arange(1, pick_total + 1, dtype=jnp.int32))
    )
    return (position, source)


def hidden_units(row_block, gate_full, up_full):
    gate_pre = jnp.einsum("esd,efd->esf", row_block, gate_full, preferred_element_type=jnp.float32)
    up_pre = jnp.einsum("esd,efd->esf", row_block, up_full, preferred_element_type=jnp.float32)
    hidden = (gate_pre * jax.nn.sigmoid(gate_pre) * up_pre).astype(jnp.bfloat16)
    return (gate_pre, up_pre, hidden)


def routed_rows(student_input, judge_output, expert_ids, route_weights, w_gate, w_up, w_down):
    tok_count, dim_model = student_input.shape
    top_picks = expert_ids.shape[1]
    exp_local = w_gate.shape[0]
    senders = lax.axis_size("expert")
    experts = exp_local * senders
    capacity = min(tok_count, tok_count * top_picks * 5 // (4 * experts))
    flat_ids = expert_ids.reshape(-1)
    position, source = slot_layout(flat_ids, experts, capacity)
    is_valid = (source > 0)[:, None]
    pick_index = jnp.maximum(source - 1, 0)
    empty_rows = jnp.zeros((), jnp.bfloat16)
    send_rows = jnp.where(is_valid, student_input[pick_index // top_picks], empty_rows).reshape(
        experts, capacity, dim_model
    )
    gate_full, up_full, down_full = (
        lax.all_gather(w_gate, "dp", axis=1, tiled=True),
        lax.all_gather(w_up, "dp", axis=1, tiled=True),
        lax.all_gather(w_down, "dp", axis=1, tiled=True),
    )
    row_block = lax.all_to_all(send_rows, "expert", split_axis=0, concat_axis=1, tiled=True)
    gate_pre, up_pre, hidden = hidden_units(row_block, gate_full, up_full)
    expert_out = jnp.einsum(
        "esf,efd->esd", hidden, down_full, preferred_element_type=jnp.float32
    ).astype(jnp.bfloat16)
    returned = lax.all_to_all(
        expert_out, "expert", split_axis=1, concat_axis=0, tiled=True
    ).reshape(experts * capacity, dim_model)
    pick_out = returned[position].reshape(tok_count, top_picks, dim_model)
    pick_wide = pick_out.astype(jnp.float32)
    mixture = jnp.sum(route_weights[:, :, None] * pick_wide, axis=1)
    residual = mixture - judge_output.astype(jnp.float32)
    route_grads = jnp.sum(pick_wide * residual[:, None, :], axis=2)
    out_grad = (
        (route_weights[:, :, None] * residual[:, None, :])
        .astype(jnp.bfloat16)
        .reshape(tok_count * top_picks, dim_model)
    )
    send_grads = jnp.where(is_valid, out_grad[pick_index], empty_rows).reshape(
        experts, capacity, dim_model
    )
    grad_block = lax.all_to_all(send_grads, "expert", split_axis=0, concat_axis=1, tiled=True)
    hidden_grad = jnp.einsum(
        "esd,efd->esf", grad_block, down_full, preferred_element_type=jnp.float32
    )
    sig_gate = jax.nn.sigmoid(gate_pre)
    gate_grad = (hidden_grad * up_pre * sig_gate * (1.0 + gate_pre * (1.0 - sig_gate))).astype(
        jnp.bfloat16
    )
    up_grad = (hidden_grad * gate_pre * sig_gate).astype(jnp.bfloat16)
    gate_part = jnp.einsum("esf,esd->efd", gate_grad, row_block, preferred_element_type=jnp.float32)
    up_part = jnp.einsum("esf,esd->efd", up_grad, row_block, preferred_element_type=jnp.float32)
    down_part = jnp.einsum("esf,esd->efd", hidden, grad_block, preferred_element_type=jnp.float32)
    grad_gate, grad_up, grad_down = (
        lax.psum_scatter(
            gate_part.astype(jnp.bfloat16), "dp", scatter_dimension=1, tiled=True
        ).astype(jnp.float32),
        lax.psum_scatter(
            up_part.astype(jnp.bfloat16), "dp", scatter_dimension=1, tiled=True
        ).astype(jnp.float32),
        lax.psum_scatter(
            down_part.astype(jnp.bfloat16), "dp", scatter_dimension=1, tiled=True
        ).astype(jnp.float32),
    )
    return (
        mixture.astype(jnp.bfloat16),
        route_grads,
        grad_gate.astype(jnp.bfloat16),
        grad_up.astype(jnp.bfloat16),
        grad_down.astype(jnp.bfloat16),
    )


UP, DOWN, ACROSS, SIBLING = range(4)
MESH = pl.DeviceIdType.MESH


def place(senders):
    me = lax.axis_index("expert")
    depth = senders // 4
    z, x, c = me // 4, (me // 2) % 2, me % 2
    return depth, z, x, c


def index_of(z, x, c):
    return z * 4 + x * 2 + c


def remote(src, dst, send_sem, recv_sem, device):
    return pltpu.make_async_remote_copy(
        src_ref=src,
        dst_ref=dst,
        send_sem=send_sem,
        recv_sem=recv_sem,
        device_id={"expert": device},
        device_id_type=MESH,
    )


def greet_all(senders):
    me = lax.axis_index("expert")
    barrier = pltpu.get_barrier_semaphore()
    for step in range(1, senders):
        other = lax.rem(me + step, senders)
        pl.semaphore_signal(barrier, inc=1, device_id={"expert": other}, device_id_type=MESH)
    pl.semaphore_wait(barrier, senders - 1)


def gather_blocks(senders, out, send_sem, recv_sem, visit):
    depth, z, x, c = place(senders)
    targets = {
        UP: lambda: index_of(z + 1, x, c),
        DOWN: lambda: index_of(z - 1, x, c),
        ACROSS: lambda: index_of(z, 1 - x, c),
        SIBLING: lambda: index_of(z, x, 1 - c),
    }

    def copy(slot, way):
        return remote(
            out.at[slot], out.at[slot], send_sem.at[slot, way], recv_sem.at[slot], targets[way]()
        )

    def arrived(slot):
        copy(slot, ACROSS).wait_recv()

    def send_on(zb, act):
        slot = index_of(zb, x, c)
        pl.when((zb <= z) & (z < depth - 1))(lambda: act(copy(slot, UP)))
        pl.when((zb >= z) & (z > 0))(lambda: act(copy(slot, DOWN)))
        act(copy(slot, ACROSS))
        act(copy(slot, SIBLING))

    near = jnp.minimum(z, depth - 1 - z)

    def layer(p):
        both_sides = z + (p + 1) // 2 * (1 - 2 * (p % 2))
        one_side = jnp.where(z < depth - 1 - z, p, depth - 1 - p)
        return jnp.where(p <= 2 * near, both_sides, one_side)

    def column_arrival(p):
        zb = layer(p)
        arrived(index_of(zb, x, c))
        send_on(zb, lambda one: one.start())

    send_on(z, lambda one: one.start())

    @pl.loop(0, 2 * depth)
    def _(step):
        p = step // 2
        turn = step % 2
        zb = layer(p)

        @pl.when(turn == 1)
        def _():
            pl.when(p == 0)(lambda: column_arrival(1))
            pl.when(p + 2 < depth)(lambda: column_arrival(p + 2))
            slot = index_of(zb, 1 - x, c)
            arrived(slot)
            copy(slot, SIBLING).start()

        xb = x + turn * (1 - 2 * x)
        arrived(index_of(zb, xb, 1 - c))
        visit(zb, xb)

    @pl.loop(0, depth)
    def _(zb):
        send_on(zb, lambda one: one.wait_send())
        copy(index_of(zb, 1 - x, c), SIBLING).wait_send()


def column_of(row):
    size = row.shape[1]
    square = (size, size)
    diagonal = lax.broadcasted_iota(jnp.int32, square, 0) == lax.broadcasted_iota(
        jnp.int32, square, 1
    )
    return jnp.sum(jnp.where(diagonal, row, 0.0), axis=1, keepdims=True)


def row_of(column):
    size = column.shape[0]
    square = (size, size)
    diagonal = lax.broadcasted_iota(jnp.int32, square, 0) == lax.broadcasted_iota(
        jnp.int32, square, 1
    )
    return jnp.sum(jnp.where(diagonal, column, 0.0), axis=0, keepdims=True)


def product(left, right, left_dim, right_dim):
    return lax.dot_general(
        left, right, (((left_dim,), (right_dim,)), ((), ())), preferred_element_type=jnp.float32
    )


def layer_kernel(
    senders,
    row_ref,
    weight_ref,
    judge_ref,
    gate_ref,
    up_ref,
    down_ref,
    mixture_ref,
    inner_ref,
    grad_gate_ref,
    grad_up_ref,
    grad_down_ref,
    rows,
    weights,
    part_ref,
    expert_out,
    hidden_all,
    gate_factor,
    up_factor,
    residual,
    inner_out,
    sums,
    sib_in,
    x_out,
    x_in,
    z_out,
    up_in,
    down_in,
    out_total,
    sib_send,
    sib_recv,
    x_send,
    x_recv,
    z_send,
    up_recv,
    down_recv,
    row_send,
    row_recv,
    residual_send,
    residual_recv,
    weight_send,
    weight_recv,
    inner_send,
    inner_recv,
):
    me = lax.axis_index("expert")
    depth, z, x, c = place(senders)
    tokens, dim_model = row_ref.shape
    rows[me] = row_ref[...]
    weights[me] = weight_ref[me]
    greet_all(senders)

    def to_each(src, dst, send, recv, act):
        @pl.loop(1, senders)
        def _(step):
            other = lax.rem(me + step, senders)
            act(src, dst, send, recv, other)

    def start_one(src, dst, send, recv, other):
        remote(src.at[other], dst.at[me], send.at[other], recv.at[me], other).start()

    def land_one(src, dst, send, recv, other):
        remote(src.at[other], dst.at[other], send.at[other], recv.at[other], other).wait_recv()

    def sent_one(src, dst, send, recv, other):
        remote(src.at[other], dst.at[me], send.at[other], recv.at[me], other).wait_send()

    weight_way = (weight_ref, weights, weight_send, weight_recv)
    inner_way = (inner_out, inner_ref, inner_send, inner_recv)
    to_each(*weight_way, start_one)

    def by_distance(act):
        for d in range(depth - 1, 0, -1):
            pl.when(z + d < depth)(functools.partial(act, z + d, UP))
            pl.when(z - d >= 0)(functools.partial(act, z - d, DOWN))
        act(z, None)

    def sib_copy(zb, xb):
        slot = zb * 2 + xb
        return remote(
            part_ref.at[index_of(zb, xb, 1 - c)],
            sib_in.at[slot],
            sib_send.at[slot],
            sib_recv.at[slot],
            index_of(z, x, 1 - c),
        )

    def x_copy(zb):
        return remote(
            x_out.at[zb], x_in.at[zb], x_send.at[zb], x_recv.at[zb], index_of(z, 1 - x, c)
        )

    def up_copy(zb):
        return remote(
            z_out.at[zb], up_in.at[zb], z_send.at[zb], up_recv.at[zb], index_of(z + 1, x, c)
        )

    def down_copy(zb):
        return remote(
            z_out.at[zb], down_in.at[zb], z_send.at[zb], down_recv.at[zb], index_of(z - 1, x, c)
        )

    def pair(ref, zb, xb):
        first = index_of(zb, xb, 0)
        return jnp.concatenate([ref[first], ref[first + 1]], axis=0)

    def pair_weights(zb, xb):
        first = index_of(zb, xb, 0)
        return jnp.concatenate(
            [column_of(weights[first][:1]), column_of(weights[first + 1][:1])], axis=0
        )

    def forward(zb, xb):
        first, at = index_of(zb, xb, 0), zb * 2 + xb
        for core in range(2):

            @pl.when(first + core != me)
            def _():
                land_one(*weight_way, first + core)

        block = pair(rows, zb, xb)
        gate_pre = product(block, gate_ref[0], 1, 1)
        up_pre = product(block, up_ref[0], 1, 1)
        sig_gate = jax.nn.sigmoid(gate_pre)
        silu = gate_pre * sig_gate
        hidden = (silu * up_pre).astype(jnp.bfloat16)
        hidden_all[at] = hidden
        up_factor[at] = silu
        gate_factor[at] = up_pre * sig_gate * (1.0 + gate_pre * (1.0 - sig_gate))
        made = product(hidden, down_ref[0], 1, 0).astype(jnp.bfloat16)
        weighted = (pair_weights(zb, xb) * made.astype(jnp.float32)).astype(jnp.bfloat16)
        for core in range(2):
            expert_out[first + core] = made[core * tokens : (core + 1) * tokens]
            part_ref[first + core] = weighted[core * tokens : (core + 1) * tokens]
        sib_copy(zb, xb).start()

    def pair_sum(zb, xb):
        mine = part_ref[index_of(zb, xb, c)].astype(jnp.float32)
        return mine + sib_in[zb * 2 + xb].astype(jnp.float32)

    def send_across(zb, way):
        sib_copy(zb, 1 - x).wait_recv()
        x_out[zb] = pair_sum(zb, 1 - x).astype(jnp.bfloat16)
        x_copy(zb).start()

    def send_along(zb, way):
        sib_copy(zb, x).wait_recv()
        x_copy(zb).wait_recv()
        out_total[...] = pair_sum(zb, x) + x_in[zb].astype(jnp.float32)
        if way != DOWN:

            @pl.when(z > 0)
            def _():
                up_copy(zb).wait_recv()
                out_total[...] += up_in[zb].astype(jnp.float32)

        if way != UP:

            @pl.when(z < depth - 1)
            def _():
                down_copy(zb).wait_recv()
                out_total[...] += down_in[zb].astype(jnp.float32)

        if way is not None:
            z_out[zb] = out_total[...].astype(jnp.bfloat16)
            (up_copy if way == UP else down_copy)(zb).start()

    def finish(zb, way):
        sib_copy(zb, 1 - x).wait_send()
        sib_copy(zb, x).wait_send()
        x_copy(zb).wait_send()
        if way is not None:
            (up_copy if way == UP else down_copy)(zb).wait_send()

    def backward(zb, xb):
        first, at = index_of(zb, xb, 0), zb * 2 + xb
        wide = pair(residual, zb, xb).astype(jnp.float32)
        out_grad = (pair_weights(zb, xb) * wide).astype(jnp.bfloat16)
        inner = jnp.sum(pair(expert_out, zb, xb).astype(jnp.float32) * wide, axis=1, keepdims=True)
        for core in range(2):
            line = row_of(inner[core * tokens : (core + 1) * tokens])
            inner_out[first + core] = jnp.broadcast_to(line, inner_out.shape[1:])

            @pl.when(first + core != me)
            def _():
                start_one(*inner_way, first + core)

        hidden_grad = product(out_grad, down_ref[0], 1, 1)
        gate_grad = (hidden_grad * gate_factor[at]).astype(jnp.bfloat16)
        up_grad = (hidden_grad * up_factor[at]).astype(jnp.bfloat16)
        block = pair(rows, zb, xb)
        sums[0] += product(gate_grad, block, 0, 0)
        sums[1] += product(up_grad, block, 0, 0)
        sums[2] += product(hidden_all[at], out_grad, 0, 0)

    gather_blocks(senders, rows, row_send, row_recv, forward)
    by_distance(send_across)
    sums[...] = jnp.zeros_like(sums)
    by_distance(send_along)
    mixture = out_total[...]
    mixture_ref[...] = mixture.astype(jnp.bfloat16)
    residual[me] = (mixture - judge_ref[...].astype(jnp.float32)).astype(jnp.bfloat16)
    gather_blocks(senders, residual, residual_send, residual_recv, backward)
    inner_ref[me] = inner_out[me]
    grad_gate_ref[0] = sums[0].astype(jnp.bfloat16)
    grad_up_ref[0] = sums[1].astype(jnp.bfloat16)
    grad_down_ref[0] = sums[2].astype(jnp.bfloat16)
    by_distance(finish)
    to_each(*weight_way, sent_one)
    to_each(*inner_way, land_one)
    to_each(*inner_way, sent_one)


def vmem_specs(count):
    return [pl.BlockSpec(memory_space=pltpu.VMEM)] * count


def whole_layer(rows, weights, judge, w_gate, w_up, w_down):
    senders = weights.shape[0]
    depth = senders // 4
    pairs = senders // 2
    block = rows.shape
    tokens = block[0]
    units = w_gate.shape[1]
    dma = pltpu.SemaphoreType.DMA

    def blocks(count):
        return pltpu.VMEM((count, *block), jnp.bfloat16)

    def unit_blocks(dtype):
        return pltpu.VMEM((pairs, 2 * tokens, units), dtype)

    grad = jax.ShapeDtypeStruct(w_gate.shape, jnp.bfloat16)
    return pl.pallas_call(
        functools.partial(layer_kernel, senders),
        out_shape=(
            jax.ShapeDtypeStruct(block, jnp.bfloat16),
            jax.ShapeDtypeStruct(weights.shape, weights.dtype),
            grad,
            grad,
            grad,
        ),
        in_specs=vmem_specs(6),
        out_specs=tuple(vmem_specs(5)),
        scratch_shapes=[
            blocks(senders),
            pltpu.VMEM(weights.shape, weights.dtype),
            blocks(senders),
            blocks(senders),
            unit_blocks(jnp.bfloat16),
            unit_blocks(jnp.float32),
            unit_blocks(jnp.float32),
            blocks(senders),
            pltpu.VMEM(weights.shape, weights.dtype),
            pltpu.VMEM((3, *w_gate.shape[1:]), jnp.float32),
            blocks(2 * depth),
            blocks(depth),
            blocks(depth),
            blocks(depth),
            blocks(depth),
            blocks(depth),
            pltpu.VMEM(block, jnp.float32),
            dma((2 * depth,)),
            dma((2 * depth,)),
            dma((depth,)),
            dma((depth,)),
            dma((depth,)),
            dma((depth,)),
            dma((depth,)),
            dma((senders, 4)),
            dma((senders,)),
            dma((senders, 4)),
            dma((senders,)),
            dma((senders,)),
            dma((senders,)),
            dma((senders,)),
            dma((senders,)),
        ],
        compiler_params=pltpu.CompilerParams(
            collective_id=0, has_side_effects=True, vmem_limit_bytes=56 << 20
        ),
    )(rows, weights, judge, w_gate, w_up, w_down)


def hand_on(*arrays):
    count = len(arrays)

    def kernel(*refs):
        done = refs[-1]
        copies = [
            pltpu.make_async_copy(refs[i], refs[count + i], done.at[i]) for i in range(count)
        ]
        for one in copies:
            one.start()
        for one in copies:
            one.wait()

    return pl.pallas_call(
        kernel,
        out_shape=tuple(jax.ShapeDtypeStruct(a.shape, a.dtype) for a in arrays),
        in_specs=[pl.BlockSpec(memory_space=pl.ANY)] * count,
        out_specs=(pl.BlockSpec(memory_space=pl.ANY),) * count,
        scratch_shapes=[pltpu.SemaphoreType.DMA((count,))],
    )(*arrays)


def dense_rows(student_input, judge_output, expert_ids, route_weights, w_gate, w_up, w_down):
    experts = lax.axis_size("expert")
    tok_count = student_input.shape[0]
    chosen = expert_ids[:, :, None] == jnp.arange(experts, dtype=jnp.int32)[None, None, :]
    dense_weights = jnp.sum(jnp.where(chosen, route_weights[:, :, None], 0.0), axis=1)
    lines = jnp.broadcast_to(dense_weights.T[:, None, :], (experts, 8, tok_count))
    mixture, inner, *grads = whole_layer(student_input, lines, judge_output, w_gate, w_up, w_down)
    route_grads = jnp.sum(jnp.where(chosen, inner[:, 0].T[:, None, :], 0.0), axis=2)
    mixture, *grads = hand_on(mixture, *grads)
    return (mixture, route_grads, *grads)


def on_device(student_input, judge_output, expert_ids, route_weights, w_gate, w_up, w_down):
    experts = w_gate.shape[0] * lax.axis_size("expert")
    senders = lax.axis_size("expert")
    alone = w_gate.shape[0] == 1 and lax.axis_size("dp") == 1 and senders % 4 == 0 and senders > 4
    dense = alone and experts <= 4 * expert_ids.shape[1]
    form = dense_rows if dense else routed_rows
    return form(student_input, judge_output, expert_ids, route_weights, w_gate, w_up, w_down)


def solution(mesh):
    placed = (
        P(("groups", "dp", "expert"), None),
        P(("groups", "dp", "expert"), None),
        P(("groups", "dp", "expert"), None),
        P(("groups", "dp", "expert"), None),
        P("expert", "dp", None),
        P("expert", "dp", None),
        P("expert", "dp", None),
    )
    return jax.shard_map(
        on_device,
        mesh=mesh,
        in_specs=placed,
        out_specs=(
            P(("groups", "dp", "expert"), None),
            P(("groups", "dp", "expert"), None),
            P(("groups", "expert"), "dp", None),
            P(("groups", "expert"), "dp", None),
            P(("groups", "expert"), "dp", None),
        ),
        check_vma=False,
    )
```
